32 devices in a mesh: ctx: 8 (over z, x), head: 4 (over y, core).
Axes of the slice: x: 2, y: 2, z: 4, core: 2. Of those that a mesh axis runs over, the one named last changes fastest.
Arguments:
- queries: bfloat16 [2048, 4096], P('ctx', 'head'), may hold values from -6 to 6
- keys: bfloat16 [2048, 2, 4096], P('ctx', None, 'head'), may hold values from -6 to 6
- values: bfloat16 [2048, 2, 4096], P('ctx', None, 'head'), may hold values from -6 to 6
- betas: float32 [2, 32, 2048], P(None, 'head', 'ctx'), may hold values from 0.02 to 1.9
- log_decay: float32 [32, 2048], P('head', 'ctx'), may hold values from -1 to 0
- segment: int32 [2048], P('ctx'), may hold values from 0 to 15, never falling along the last dimension, each value on 1 to 1024 neighbouring positions
- gain: float32 [4096], P('head'), may hold values from 0.1 to 1.9
- out_weight: bfloat16 [4096, 4096], P('head'), may hold values from -0.125 to 0.125
Outputs:
- mixed: bfloat16 [2048, 4096], P('ctx', 'head')
The draws below stay inside these ranges and needn't reach their ends.
Inputs may be any that keep to these rules, and one draw needn't show every extreme that they name: `segment`: document numbers never fall along the context; every document has 1 to 1024 tokens and one has exactly 1024.
All inputs are finite; a program needn't handle non-finite values.
Results may differ from the reference program's by a relative error of at most 0.0049.
Values sent between devices are 32-bit elements; how exact they have to be, the bound alone decides.
A program may use at most 192 MiB of HBM per device.

```python
import math
import jax
import jax.numpy as jnp
import numpy as np
from jax import lax

D = 4096
H = 32
DK = 128
DV = 128
GROUP = 64
TOK_DEV = 256
TOTAL_POSITIONS = 2048
DOCUMENT_LIMIT = 1024
DOCS = 16


def slow_heads(key, slow_count):
    order = jax.random.permutation(jax.random.fold_in(key, 101), H)
    return order < slow_count


def draw_keys(key, part):
    blocks = TOTAL_POSITIONS // GROUP
    shared_key, noise_key = jax.random.split(jax.random.fold_in(key, 17))
    shared = jnp.clip(jax.random.normal(shared_key, (blocks, 1, 1, H, DK), jnp.float32), -4.0, 4.0)
    noise = jnp.clip(jax.random.normal(noise_key, (blocks, GROUP, 2, H, DK), jnp.float32), -4.0, 4.0)
    combined = 0.6 * shared + 0.8 * noise
    return combined.reshape(TOTAL_POSITIONS, 2, H * DK).astype(jnp.bfloat16)


def draw_betas(key, part):
    slow_count = H // 2
    fast_low = 0.2
    upper_fast_rate = 1.8
    slow = slow_heads(key, slow_count)
    first, second = jax.random.split(jax.random.fold_in(key, 5))
    weak = jnp.exp(jax.random.uniform(first, (2, H, TOTAL_POSITIONS), jnp.float32, math.log(0.02), math.log(0.049)))
    strong = jax.random.uniform(second, (2, H, TOTAL_POSITIONS), jnp.float32, fast_low, upper_fast_rate)
    return jnp.where(slow[None, :, None], weak, strong).astype(jnp.float32)


def draw_log_decay(key, part):
    slow_count = H // 2
    slow = slow_heads(key, slow_count)
    packed_keys = jax.random.split(jax.random.fold_in(key, 9), 6)
    slow_rate = jnp.exp(jax.random.uniform(packed_keys[0], (H,), jnp.float32, math.log(2e-05), math.log(0.0001)))
    fast_rate = jnp.exp(jax.random.uniform(packed_keys[1], (H,), jnp.float32, math.log(0.001), math.log(0.004)))
    base = jnp.where(slow, slow_rate, fast_rate)
    blocks = TOTAL_POSITIONS // TOK_DEV
    factor = jnp.exp(jax.random.uniform(packed_keys[2], (H, blocks), jnp.float32, -math.log(2.0), math.log(2.0)))
    factor = jnp.repeat(factor, TOK_DEV, axis=1)
    rough = jax.random.uniform(packed_keys[3], (H, TOTAL_POSITIONS), jnp.float32, 0.5, 1.5)
    token_group = jax.random.uniform(packed_keys[4], (TOTAL_POSITIONS,), jnp.float32) < 2.0 / DOCUMENT_LIMIT
    token_total = jax.random.uniform(packed_keys[5], (TOTAL_POSITIONS,), jnp.float32, 0.22, 0.69)
    forget_factor = jnp.where(token_group, token_total, jnp.zeros_like(token_total))
    return (-(base[:, None] * factor * rough) - forget_factor[None, :]).astype(jnp.float32)


def spiked(entries, own_key, source, target, shards_of, factor):
    def block_of(axis_at):
        return (jnp.arange(entries.shape[axis_at]) // (entries.shape[axis_at] // shards_of)).reshape((-1,) + (1,) * (entries.ndim - 1 - axis_at))

    first = jax.random.permutation(own_key, shards_of)[block_of(target)]
    second = (block_of(target) + shards_of // 2) % shards_of
    return jnp.where((block_of(source) == first) | (block_of(source) == second), factor * entries, entries)


def steps_of(stream_key, shape, shards, low, top_value):
    loudness, own = 1.0, jax.random.fold_in(stream_key, 6)
    for position, blocks in shards:
        draws = jnp.exp(jax.random.uniform(jax.random.fold_in(own, position), (blocks,), jnp.float32, low / len(shards), top_value / len(shards)))
        loudness = loudness * jnp.repeat(draws, shape[position] // blocks).reshape([-1 if axis == position else 1 for axis in range(len(shape))])
    return loudness


def profile(count, total, limit, slope):
    portions = [(1 << 20) // math.isqrt(rank ** slope) + 1 for rank in range(2, count + 1)]
    surplus, holding = total - limit - (count - 1), [1] * (count - 1)
    while surplus > 0:
        free = [i for i in range(count - 1) if holding[i] < limit]
        pool, budget = sum([portions[i] for i in free]), surplus
        for i in free:
            more = min(limit - holding[i], max(1, budget * portions[i] // pool), surplus)
            holding[i] = holding[i] + more
            surplus = surplus - more
    return np.array([limit] + holding)


def ragged_sizes(key, number_of, total, most, slope):
    if number_of == 2:
        one = jax.random.randint(key, (), max(1, total - most), min(most, total - 1) + 1)
        return jnp.stack([one, total - one])
    tallies = jnp.asarray(profile(number_of, total, most, slope), jnp.int32)
    twos = (number_of - 1) // 2
    source_of, receiver = tallies[1:1 + 2 * twos:2], tallies[2:2 + 2 * twos:2]
    slack = jnp.minimum(source_of - 1, most - receiver)
    moved = jax.random.randint(jax.random.fold_in(key, 1), (twos,), 0, 1 << 20) % (slack + 1)
    tallies = tallies.at[1:1 + 2 * twos:2].set(source_of - moved).at[2:2 + 2 * twos:2].set(receiver + moved)
    return tallies[jax.random.permutation(jax.random.fold_in(key, 2), number_of)]


def normal_values(rng, extent, scale, most, pieces=(), dtype=jnp.bfloat16):
    level = steps_of(rng, extent, pieces, -0.22, 0.18) if pieces else 1.0
    drawn = jax.random.normal(rng, extent, jnp.float32) * scale * level
    return jnp.minimum(jnp.maximum(drawn, -most), most).astype(dtype)


def gaussian_with(own_key, shape, scale, limit, shards, heavy, held_as=jnp.bfloat16):
    array = scale * jax.random.normal(own_key, shape, jnp.float32)
    if shards:
        array = array * steps_of(own_key, shape, shards, -0.22, 0.18)
    return jnp.clip(spiked(array, jax.random.fold_in(own_key, 3), *heavy), -limit, limit).astype(held_as)


def setup_inputs(seed: int = 0) -> dict:
    arg_keys = jax.random.split(jax.random.key(seed), 9)
    return {
        "queries": normal_values(arg_keys[0], (TOTAL_POSITIONS, H * DK), 1.0, 6.0, ((0, 8), (1, 4))),
        "keys": draw_keys(jax.random.fold_in(arg_keys[8], 71), 0),
        "values": normal_values(arg_keys[2], (TOTAL_POSITIONS, 2, H * DV), 1.0, 6.0, ((0, 8), (2, 4))),
        "betas": draw_betas(jax.random.fold_in(arg_keys[8], 71), 0),
        "log_decay": draw_log_decay(jax.random.fold_in(arg_keys[8], 71), 0),
        "segment": jnp.searchsorted(jnp.cumsum(ragged_sizes(arg_keys[5], DOCS, TOTAL_POSITIONS, DOCUMENT_LIMIT, 2)), jnp.arange(TOTAL_POSITIONS), side="right").astype(jnp.int32),
        "gain": jnp.clip(1.0 + 0.18 * jax.random.normal(arg_keys[6], (H * DV,), jnp.float32), 0.1, 1.9),
        "out_weight": gaussian_with(arg_keys[7], (H * DV, D), (H * DV) ** -0.5, 0.125, ((0, 4),), (0, 1, 4, 2.0)),
    }


def unit_rows(matrix):
    return matrix / jnp.sqrt(lax.optimization_barrier(jnp.sum(matrix * matrix, axis=-1, keepdims=True)) + 1e-06)

def reference(queries, keys, values, betas, log_decay, segment, gain, out_weight):
    positions = queries.shape[0]
    highest = lax.Precision.HIGHEST
    query_unit = unit_rows(queries.astype(jnp.float32).reshape(positions, H, DK))
    key_unit = unit_rows(keys.astype(jnp.float32).reshape(positions, 2, H, DK))
    value_rows = values.astype(jnp.float32).reshape(positions, 2, H, DV)
    strengths = jnp.transpose(betas, (2, 0, 1))
    decay = jnp.exp(log_decay).T
    previous = jnp.concatenate([jnp.full((1,), -1, jnp.int32), segment[:-1].astype(jnp.int32)])
    retain_all = jnp.where((segment.astype(jnp.int32) == previous)[:, None], decay, jnp.zeros_like(decay))

    def advance(state, inputs):
        retain, query_row, key_pair, value_pair, strength_pair = inputs
        state = state * retain[:, None, None]
        for which in range(2):
            guess = jnp.einsum('hvk,hk->hv', state, key_pair[which], precision=highest)
            update = jnp.einsum('hv,hk->hvk', value_pair[which] - guess, key_pair[which], precision=highest)
            state = state + strength_pair[which][:, None, None] * update
        reading = jnp.einsum('hvk,hk->hv', state, query_row, precision=highest)
        return (state, reading)
    blank_state = jnp.zeros((H, DV, DK), jnp.float32)
    final_state, attended = lax.scan(advance, blank_state, (retain_all, query_unit, key_unit, value_rows, strengths))
    inverse_rms = 1.0 / jnp.sqrt(lax.optimization_barrier(jnp.mean(attended * attended, axis=-1, keepdims=True)) + 1e-06)
    normed = ((attended * inverse_rms).reshape(positions, H * DV) * gain[None, :]).astype(jnp.bfloat16)
    return jnp.dot(normed, out_weight, preferred_element_type=jnp.float32).astype(jnp.bfloat16)
```

```python
import functools
import jax
import jax.numpy as jnp
from jax import lax
from jax.experimental import pallas as pl
from jax.experimental.pallas import tpu as pltpu
from jax.sharding import PartitionSpec as P

DK = 128
DV = 128
GROUP = 64
ROWS = 2 * GROUP
HEADS_STEP = 2
F32 = jnp.float32
BF16 = jnp.bfloat16


def halves(a):
    if a.dtype == BF16:
        return a, None
    hi = a.astype(BF16)
    return hi, (a - hi.astype(F32)).astype(BF16)


def one(a, b):
    return jnp.dot(a, b, preferred_element_type=F32)


def mul(a, b):
    a_hi, a_lo = a if isinstance(a, tuple) else halves(a)
    b_hi, b_lo = b if isinstance(b, tuple) else halves(b)
    out = one(a_hi, b_hi)
    if a_lo is not None:
        out = out + one(a_lo, b_hi)
    if b_lo is not None:
        out = out + one(a_hi, b_lo)
    return out


def exact(a, b):
    return lax.dot_general(
        a, b, (((1,), (0,)), ((), ())), precision=lax.Precision.HIGHEST, preferred_element_type=F32
    )


def local_kernel(q_ref, k_ref, v_ref, beta_ref, log_ref, seg_ref, map_ref, add_ref, mapped_ref, local_ref):
    step = pl.program_id(0)
    blocks = q_ref.shape[0] // GROUP
    row = lax.broadcasted_iota(jnp.int32, (ROWS, ROWS), 0)
    col = lax.broadcasted_iota(jnp.int32, (ROWS, ROWS), 1)
    row_tok = lax.broadcasted_iota(jnp.int32, (GROUP, ROWS), 0)
    col_tok = lax.broadcasted_iota(jnp.int32, (GROUP, ROWS), 1)
    eye = (row == col).astype(F32)
    summing = ((row < GROUP) & (row <= col // 2)).astype(F32)
    spreading = ((row < GROUP) & (row == col // 2)).astype(F32)
    weaving = jnp.where(
        row < GROUP, (col == 2 * row).astype(F32), (col == 2 * (row - GROUP) + 1).astype(F32)
    )
    units = []
    for which in range(HEADS_STEP):
        head = step * HEADS_STEP + which
        logs = log_ref[pl.ds(head, 1), :]
        first = beta_ref[0, pl.ds(head, 1), :]
        second = beta_ref[1, pl.ds(head, 1), :]
        segs = seg_ref[...].astype(F32)
        for block in range(blocks):
            units.append((which, block, logs, first, second, segs))

    prepared = []
    for which, block, logs, first, second, segs in units:
        toks = slice(block * GROUP, (block + 1) * GROUP)
        zero = jnp.zeros((1, GROUP), F32)
        packed = jnp.concatenate(
            [
                jnp.concatenate([logs[:, toks], zero], axis=1),
                jnp.concatenate([first[:, toks], second[:, toks]], axis=1),
                jnp.concatenate([segs[:, toks], zero], axis=1),
                jnp.zeros((5, ROWS), F32),
            ],
            axis=0,
        )
        cum_row = exact(packed, summing)[0:1]
        beta_row = exact(packed, weaving)[1:2]
        seg_row = exact(packed, spreading)[2:3]
        columns = jnp.transpose(
            jnp.concatenate([cum_row, beta_row, seg_row, jnp.zeros((ROWS - 3, ROWS), F32)], axis=0)
        )
        cum_col, beta_col, seg_col = columns[:, 0:1], columns[:, 1:2], columns[:, 2:3]
        tok_columns = jnp.transpose(
            jnp.concatenate(
                [
                    exact(packed, ((row < GROUP) & (row <= col)).astype(F32))[0:1],
                    packed[2:3],
                    jnp.zeros((ROWS - 2, ROWS), F32),
                ],
                axis=0,
            )
        )[:GROUP]
        cum_tok, seg_tok = tok_columns[:, 0:1], tok_columns[:, 1:2]
        start = segs[:, 0:1] if block == 0 else segs[:, block * GROUP - 1 : block * GROUP]
        last_seg = segs[:, (block + 1) * GROUP - 1 : (block + 1) * GROUP]
        cum_last = cum_row[:, ROWS - 1 : ROWS]

        lanes = slice(which * DK, (which + 1) * DK)
        keys = k_ref[block * ROWS : (block + 1) * ROWS, lanes]
        query = q_ref[toks, lanes]
        keys_t = jnp.transpose(keys.astype(F32)).astype(BF16)
        both = one(jnp.concatenate([keys, query], axis=0), keys_t)
        gram, meets = both[:ROWS], both[ROWS:]
        diagonal = gram * eye
        inv_row = lax.rsqrt(jnp.sum(diagonal, axis=0, keepdims=True) + 1e-06)
        inv_col = lax.rsqrt(jnp.sum(diagonal, axis=1, keepdims=True) + 1e-06)
        query_f = query.astype(F32)
        inv_query = lax.rsqrt(jnp.sum(query_f * query_f, axis=1, keepdims=True) + 1e-06)
        lower = jnp.where(
            (seg_col == seg_row) & (row > col),
            (beta_col * inv_col) * jnp.exp(cum_col - cum_row) * (gram * inv_row),
            0.0,
        )
        scores = jnp.where(
            (seg_tok == seg_row) & (col_tok <= 2 * row_tok + 1),
            inv_query * jnp.exp(cum_tok - cum_row) * (meets * inv_row),
            0.0,
        )
        entry_row = jnp.where(seg_row == start, jnp.exp(cum_row), 0.0)
        entry_tok = jnp.where(seg_tok == start, jnp.exp(cum_tok), 0.0)
        tail_col = jnp.where(seg_col == last_seg, jnp.exp(cum_last - cum_col), 0.0)
        tail_entry = jnp.where(last_seg == start, jnp.exp(cum_last), 0.0)
        prepared.append(
            dict(
                keys=keys,
                keys_t=keys_t,
                lower=lower,
                scores=scores,
                value_scale=beta_row,
                key_scale=beta_row * entry_row * inv_row,
                tail=tail_col * inv_col,
                tail_entry=tail_entry,
                reach=(entry_tok * inv_query) * query_f,
            )
        )

    inverses = [eye - jnp.where(row // 2 == col // 2, p["lower"], 0.0) for p in prepared]
    size = 2
    while size < ROWS:
        below = (row // (2 * size) == col // (2 * size)) & (row // size > col // size)
        split = [halves(x) for x in inverses]
        inner = [mul(jnp.where(below, p["lower"], 0.0), s) for p, s in zip(prepared, split)]
        inverses = [x - mul(s, i) for x, s, i in zip(inverses, split, inner)]
        size *= 2

    solved = []
    for (which, block, *_), p, x in zip(units, prepared, inverses):
        values = v_ref[block * ROWS : (block + 1) * ROWS, which * DV : (which + 1) * DV]
        key_mix = mul(x * p["key_scale"], p["keys"])
        pseudo = mul(x * p["value_scale"], values)
        solved.append(jnp.concatenate([key_mix, pseudo], axis=1))
    reads = [mul(p["scores"], s) for p, s in zip(prepared, solved)]
    moves = [mul(p["keys_t"], s * p["tail"]) for p, s in zip(prepared, solved)]
    running = [None] * HEADS_STEP
    for block in range(blocks):
        for which in range(HEADS_STEP):
            at = which * blocks + block
            p, toks = prepared[at], slice(block * GROUP, (block + 1) * GROUP)
            reach = p["reach"] - reads[at][:, :DK]
            block_map = p["tail_entry"] * eye - moves[at][:, :DK]
            if block == 0:
                mapped, local = reach, reads[at][:, DK:]
                running[which] = jnp.concatenate([block_map, moves[at][:, DK:]], axis=1)
            else:
                before = halves(running[which])
                out = mul(reach, before)
                mapped, local = out[:, :DK], out[:, DK:] + reads[at][:, DK:]
                turned = mul(block_map, before)
                running[which] = jnp.concatenate(
                    [turned[:, :DK], turned[:, DK:] + moves[at][:, DK:]], axis=1
                )
            mapped_ref[which, toks, :] = mapped
            local_ref[which, toks, :] = local
    for which in range(HEADS_STEP):
        map_ref[which] = running[which][:, :DK]
        add_ref[which] = running[which][:, DK:]


def local_parts(queries, keys, values, betas, log_decay, segment):
    tok_local = queries.shape[0]
    heads_local = betas.shape[1]
    lanes = HEADS_STEP * DK
    whole = lambda *shape: pl.BlockSpec(shape, lambda h: (0,) * len(shape))
    per_head = lambda rows: pl.BlockSpec((HEADS_STEP, rows, DK), lambda h: (h, 0, 0))
    shape = lambda rows: jax.ShapeDtypeStruct((heads_local, rows, DK), F32)
    return pl.pallas_call(
        local_kernel,
        grid=(heads_local // HEADS_STEP,),
        in_specs=[
            pl.BlockSpec((tok_local, lanes), lambda h: (0, h)),
            pl.BlockSpec((2 * tok_local, lanes), lambda h: (0, h)),
            pl.BlockSpec((2 * tok_local, lanes), lambda h: (0, h)),
            whole(2, heads_local, tok_local),
            whole(heads_local, tok_local),
            whole(1, tok_local),
        ],
        out_specs=[per_head(DK), per_head(DK), per_head(tok_local), per_head(tok_local)],
        out_shape=[shape(DK), shape(DK), shape(tok_local), shape(tok_local)],
        compiler_params=pltpu.CompilerParams(vmem_limit_bytes=48 * 1024 * 1024),
        cost_estimate=pl.CostEstimate(flops=12 * 10**9, bytes_accessed=8 * 10**6, transcendentals=10**6),
        name="local_blocks",
    )(
        queries,
        keys.reshape(2 * tok_local, -1),
        values.reshape(2 * tok_local, -1),
        betas,
        log_decay,
        segment.reshape(1, tok_local),
    )


def shifted(value, axis, steps):
    count = lax.axis_size(axis)
    return lax.ppermute(value, axis, [(source, source + steps) for source in range(count - steps)])


def shards(queries, keys, values, betas, log_decay, segment, gain, out_weight):
    tok_local = queries.shape[0]
    heads_local = betas.shape[1]
    before = shifted(segment[tok_local - 1 :], "ctx", 1)
    maps, adds, mapped, local_out = local_parts(queries, keys, values, betas, log_decay, segment)
    linked = ((before[0] == segment[0]) & (lax.axis_index("ctx") > 0)).astype(F32)
    turns = min(8, lax.axis_size("ctx") // 2)
    arrived = None
    leaving = adds
    for _ in range(turns):
        arrived = shifted(leaving, "ctx", 1) * linked
        leaving = jnp.einsum("hab,hbv->hav", maps, arrived, precision=lax.Precision.HIGH) + adds
    attended = local_out + jnp.einsum(
        "hik,hkv->hiv", mapped, arrived, precision=lax.Precision.HIGH
    )
    attended = jnp.transpose(attended, (1, 0, 2))
    inverse_rms = 1.0 / jnp.sqrt(jnp.mean(attended * attended, axis=-1, keepdims=True) + 1e-06)
    normed = ((attended * inverse_rms).reshape(tok_local, heads_local * DV) * gain[None, :]).astype(BF16)
    terms = jnp.dot(normed, out_weight, preferred_element_type=F32)
    return lax.psum_scatter(terms, "head", scatter_dimension=1, tiled=True).astype(BF16)


def solution(mesh):
    return jax.shard_map(
        shards,
        mesh=mesh,
        in_specs=(
            P("ctx", "head"),
            P("ctx", None, "head"),
            P("ctx", None, "head"),
            P(None, "head", "ctx"),
            P("head", "ctx"),
            P("ctx"),
            P("head"),
            P("head", None),
        ),
        out_specs=P("ctx", "head"),
        check_vma=False,
    )
```

```python
import functools
import jax
import jax.numpy as jnp
from jax import lax
from jax.experimental import pallas as pl
from jax.experimental.pallas import tpu as pltpu
from jax.sharding import PartitionSpec as P

DK = 128
DV = 128
GROUP = 64
ROWS = 2 * GROUP
HEADS_STEP = 2
F32 = jnp.float32
BF16 = jnp.bfloat16


def halves(a):
    if a.dtype == BF16:
        return a, None
    hi = a.astype(BF16)
    return hi, (a - hi.astype(F32)).astype(BF16)


def one(a, b):
    return jnp.dot(a, b, preferred_element_type=F32)


def mul(a, b):
    a_hi, a_lo = a if isinstance(a, tuple) else halves(a)
    b_hi, b_lo = b if isinstance(b, tuple) else halves(b)
    out = one(a_hi, b_hi)
    if a_lo is not None:
        out = out + one(a_lo, b_hi)
    if b_lo is not None:
        out = out + one(a_hi, b_lo)
    return out


def exact(a, b):
    return lax.dot_general(
        a, b, (((1,), (0,)), ((), ())), precision=lax.Precision.HIGHEST, preferred_element_type=F32
    )


def local_kernel(
    q_ref, k_ref, v_ref, beta_ref, log_ref, seg_ref, map_ref, add_ref, mapped_ref, local_ref, edge_ref
):
    step = pl.program_id(0)
    blocks = q_ref.shape[0] // GROUP
    row = lax.broadcasted_iota(jnp.int32, (ROWS, ROWS), 0)
    col = lax.broadcasted_iota(jnp.int32, (ROWS, ROWS), 1)
    row_tok = lax.broadcasted_iota(jnp.int32, (GROUP, ROWS), 0)
    col_tok = lax.broadcasted_iota(jnp.int32, (GROUP, ROWS), 1)
    eye = (row == col).astype(F32)
    summing = ((row < GROUP) & (row <= col // 2)).astype(F32)
    spreading = ((row < GROUP) & (row == col // 2)).astype(F32)
    weaving = jnp.where(
        row < GROUP, (col == 2 * row).astype(F32), (col == 2 * (row - GROUP) + 1).astype(F32)
    )
    units = []
    for which in range(HEADS_STEP):
        head = step * HEADS_STEP + which
        logs = log_ref[pl.ds(head, 1), :]
        first = beta_ref[0, pl.ds(head, 1), :]
        second = beta_ref[1, pl.ds(head, 1), :]
        segs = seg_ref[...].astype(F32)
        for block in range(blocks):
            units.append((which, block, logs, first, second, segs))

    prepared = []
    for which, block, logs, first, second, segs in units:
        toks = slice(block * GROUP, (block + 1) * GROUP)
        zero = jnp.zeros((1, GROUP), F32)
        packed = jnp.concatenate(
            [
                jnp.concatenate([logs[:, toks], zero], axis=1),
                jnp.concatenate([first[:, toks], second[:, toks]], axis=1),
                jnp.concatenate([segs[:, toks], zero], axis=1),
                jnp.zeros((5, ROWS), F32),
            ],
            axis=0,
        )
        cum_row = exact(packed, summing)[0:1]
        beta_row = exact(packed, weaving)[1:2]
        seg_row = exact(packed, spreading)[2:3]
        columns = jnp.transpose(
            jnp.concatenate([cum_row, beta_row, seg_row, jnp.zeros((ROWS - 3, ROWS), F32)], axis=0)
        )
        cum_col, beta_col, seg_col = columns[:, 0:1], columns[:, 1:2], columns[:, 2:3]
        tok_columns = jnp.transpose(
            jnp.concatenate(
                [
                    exact(packed, ((row < GROUP) & (row <= col)).astype(F32))[0:1],
                    packed[2:3],
                    jnp.zeros((ROWS - 2, ROWS), F32),
                ],
                axis=0,
            )
        )[:GROUP]
        cum_tok, seg_tok = tok_columns[:, 0:1], tok_columns[:, 1:2]
        start = segs[:, 0:1] if block == 0 else segs[:, block * GROUP - 1 : block * GROUP]
        last_seg = segs[:, (block + 1) * GROUP - 1 : (block + 1) * GROUP]
        cum_last = cum_row[:, ROWS - 1 : ROWS]

        lanes = slice(which * DK, (which + 1) * DK)
        keys = k_ref[block * ROWS : (block + 1) * ROWS, lanes]
        query = q_ref[toks, lanes]
        keys_t = jnp.transpose(keys.astype(F32)).astype(BF16)
        both = one(jnp.concatenate([keys, query], axis=0), keys_t)
        gram, meets = both[:ROWS], both[ROWS:]
        diagonal = gram * eye
        inv_row = lax.rsqrt(jnp.sum(diagonal, axis=0, keepdims=True) + 1e-06)
        inv_col = lax.rsqrt(jnp.sum(diagonal, axis=1, keepdims=True) + 1e-06)
        query_f = query.astype(F32)
        inv_query = lax.rsqrt(jnp.sum(query_f * query_f, axis=1, keepdims=True) + 1e-06)
        lower = jnp.where(
            (seg_col == seg_row) & (row > col),
            (beta_col * inv_col) * jnp.exp(cum_col - cum_row) * (gram * inv_row),
            0.0,
        )
        scores = jnp.where(
            (seg_tok == seg_row) & (col_tok <= 2 * row_tok + 1),
            inv_query * jnp.exp(cum_tok - cum_row) * (meets * inv_row),
            0.0,
        )
        entry_row = jnp.where(seg_row == start, jnp.exp(cum_row), 0.0)
        entry_tok = jnp.where(seg_tok == start, jnp.exp(cum_tok), 0.0)
        tail_col = jnp.where(seg_col == last_seg, jnp.exp(cum_last - cum_col), 0.0)
        tail_entry = jnp.where(last_seg == start, jnp.exp(cum_last), 0.0)
        prepared.append(
            dict(
                keys=keys,
                keys_t=keys_t,
                lower=lower,
                scores=scores,
                value_scale=beta_row,
                key_scale=beta_row * entry_row * inv_row,
                tail=tail_col * inv_col,
                tail_entry=tail_entry,
                reach=(entry_tok * inv_query) * query_f,
            )
        )

    inverses = [eye - jnp.where(row // 2 == col // 2, p["lower"], 0.0) for p in prepared]
    size = 2
    while size < ROWS:
        below = (row // (2 * size) == col // (2 * size)) & (row // size > col // size)
        split = [halves(x) for x in inverses]
        inner = [mul(jnp.where(below, p["lower"], 0.0), s) for p, s in zip(prepared, split)]
        inverses = [x - mul(s, i) for x, s, i in zip(inverses, split, inner)]
        size *= 2

    solved = []
    for (which, block, *_), p, x in zip(units, prepared, inverses):
        values = v_ref[block * ROWS : (block + 1) * ROWS, which * DV : (which + 1) * DV]
        key_mix = mul(x * p["key_scale"], p["keys"])
        pseudo = mul(x * p["value_scale"], values)
        solved.append(jnp.concatenate([key_mix, pseudo], axis=1))
    reads = [mul(p["scores"], s) for p, s in zip(prepared, solved)]
    moves = [mul(p["keys_t"], s * p["tail"]) for p, s in zip(prepared, solved)]
    running = [None] * HEADS_STEP
    for block in range(blocks):
        for which in range(HEADS_STEP):
            at = which * blocks + block
            p, toks = prepared[at], slice(block * GROUP, (block + 1) * GROUP)
            reach = p["reach"] - reads[at][:, :DK]
            block_map = p["tail_entry"] * eye - moves[at][:, :DK]
            if block == 0:
                mapped, local = reach, reads[at][:, DK:]
                running[which] = jnp.concatenate([block_map, moves[at][:, DK:]], axis=1)
            else:
                before = halves(running[which])
                out = mul(reach, before)
                mapped, local = out[:, :DK], out[:, DK:] + reads[at][:, DK:]
                turned = mul(block_map, before)
                running[which] = jnp.concatenate(
                    [turned[:, :DK], turned[:, DK:] + moves[at][:, DK:]], axis=1
                )
            mapped_ref[which, toks, :] = mapped
            local_ref[which, toks, :] = local
    for which in range(HEADS_STEP):
        map_ref[which] = running[which][:, :DK]
        add_ref[which] = running[which][:, DK:]
    segs = seg_ref[...].astype(F32)
    edge_ref[0] = jnp.broadcast_to(segs[:, 0:1], (8, 128))
    edge_ref[1] = jnp.broadcast_to(segs[:, segs.shape[1] - 1 :], (8, 128))


def local_parts(queries, keys, values, betas, log_decay, segment):
    tok_local = queries.shape[0]
    heads_local = betas.shape[1]
    lanes = HEADS_STEP * DK
    whole = lambda *shape: pl.BlockSpec(shape, lambda h: (0,) * len(shape))
    per_head = lambda rows: pl.BlockSpec((HEADS_STEP, rows, DK), lambda h: (h, 0, 0))
    shape = lambda rows: jax.ShapeDtypeStruct((heads_local, rows, DK), F32)
    return pl.pallas_call(
        local_kernel,
        grid=(heads_local // HEADS_STEP,),
        in_specs=[
            pl.BlockSpec((tok_local, lanes), lambda h: (0, h)),
            pl.BlockSpec((2 * tok_local, lanes), lambda h: (0, h)),
            pl.BlockSpec((2 * tok_local, lanes), lambda h: (0, h)),
            whole(2, heads_local, tok_local),
            whole(heads_local, tok_local),
            whole(1, tok_local),
        ],
        out_specs=[per_head(DK), per_head(DK), per_head(tok_local), per_head(tok_local), whole(2, 8, 128)],
        out_shape=[shape(DK), shape(DK), shape(tok_local), shape(tok_local)]
        + [jax.ShapeDtypeStruct((2, 8, 128), F32)],
        compiler_params=pltpu.CompilerParams(vmem_limit_bytes=48 * 1024 * 1024),
        cost_estimate=pl.CostEstimate(flops=12 * 10**9, bytes_accessed=8 * 10**6, transcendentals=10**6),
        name="local_blocks",
    )(
        queries,
        keys.reshape(2 * tok_local, -1),
        values.reshape(2 * tok_local, -1),
        betas,
        log_decay,
        segment.reshape(1, tok_local),
    )


MESH = pl.DeviceIdType.MESH
CHUNK = 256


def finish_kernel(
    map_ref, add_ref, mapped_ref, local_ref, edge_ref, gain_ref, weight_ref, out_ref,
    weight, normed, states, leaving, seg_in, outgoing, incoming, total, summed,
    weight_sem, seg_send, seg_recv, chain_send, chain_recv, pair_send, pair_recv, far_send, far_recv,
):
    place, places = lax.axis_index("ctx"), lax.axis_size("ctx")
    mine = lax.axis_index("head")
    heads = map_ref.shape[0]
    width = out_ref.shape[1]
    chunks = width // CHUNK
    beside = mine + 1 - 2 * lax.rem(mine, 2)
    across = lax.rem(mine + 2, 4)
    diagonal = 3 - mine
    after, before = place + 1, place - 1
    has_after, has_before = place < places - 1, place > 0

    fetch = pltpu.make_async_copy(weight_ref, weight, weight_sem)
    fetch.start()
    barrier = pltpu.get_barrier_semaphore()
    for partner in (beside, across):
        pl.semaphore_signal(barrier, inc=1, device_id=(place, partner), device_id_type=MESH)

    @pl.when(has_after)
    def _():
        pl.semaphore_signal(barrier, inc=1, device_id=(after, mine), device_id_type=MESH)

    @pl.when(has_before)
    def _():
        pl.semaphore_signal(barrier, inc=1, device_id=(before, mine), device_id_type=MESH)

    pl.semaphore_wait(barrier, 2 + has_after.astype(jnp.int32) + has_before.astype(jnp.int32))

    seg_copy = pltpu.make_async_remote_copy(
        src_ref=edge_ref.at[1], dst_ref=seg_in, send_sem=seg_send, recv_sem=seg_recv,
        device_id=(after, mine), device_id_type=MESH,
    )

    def state_copy(head):
        return pltpu.make_async_remote_copy(
            src_ref=leaving.at[head], dst_ref=states.at[head],
            send_sem=chain_send.at[head], recv_sem=chain_recv.at[head],
            device_id=(after, mine), device_id_type=MESH,
        )

    def attend(head, state):
        attended = local_ref[head]
        if state is not None:
            attended = attended + mul(mapped_ref[head], state)
        inverse_rms = 1.0 / jnp.sqrt(jnp.mean(attended * attended, axis=-1, keepdims=True) + 1e-06)
        lanes = pl.ds(pl.multiple_of(head * DV, DV), DV)
        normed[:, lanes] = (attended * inverse_rms * gain_ref[:, lanes]).astype(BF16)

    @pl.when(place == 0)
    def _():
        seg_copy.start()

        def first(head, carry):
            leaving[head] = add_ref[head]
            state_copy(head).start()
            return carry

        lax.fori_loop(0, heads, first, 0)

        def read(head, carry):
            attend(head, None)
            return carry

        lax.fori_loop(0, heads, read, 0)

    @pl.when(has_before)
    def _():
        @pl.when(has_after)
        def _():
            seg_copy.start()

        seg_copy.wait_recv()
        linked = seg_in[0:1, :] == edge_ref[0, 0:1, :]

        def link(head, carry):
            state_copy(head).wait_recv()
            state = halves(jnp.where(linked, states[head], 0.0))

            @pl.when(has_after)
            def _():
                leaving[head] = mul(map_ref[head], state) + add_ref[head]
                state_copy(head).start()

            attend(head, state)
            return carry

        lax.fori_loop(0, heads, link, 0)

    fetch.wait()

    def product(owner, chunk):
        lanes = pl.ds(pl.multiple_of(owner * width + chunk * CHUNK, CHUNK), CHUNK)
        return one(normed[...], weight[:, lanes])

    def pair_copy(near, chunk):
        return pltpu.make_async_remote_copy(
            src_ref=outgoing.at[near, chunk], dst_ref=incoming.at[near, chunk],
            send_sem=pair_send.at[near, chunk], recv_sem=pair_recv.at[near, chunk],
            device_id=(place, beside), device_id_type=MESH,
        )

    def far_copy(chunk):
        return pltpu.make_async_remote_copy(
            src_ref=total.at[0, chunk], dst_ref=summed.at[chunk],
            send_sem=far_send.at[chunk], recv_sem=far_recv.at[chunk],
            device_id=(place, across), device_id_type=MESH,
        )

    for near, theirs, ours in ((0, diagonal, across), (1, beside, mine)):

        def give(chunk, carry):
            outgoing[near, chunk] = product(theirs, chunk)
            pair_copy(near, chunk).start()
            return carry

        def take(chunk, carry):
            part = product(ours, chunk)
            pair_copy(near, chunk).wait_recv()
            total[near, chunk] = part + incoming[near, chunk]
            if near == 0:
                far_copy(chunk).start()
            return carry

        lax.fori_loop(0, chunks, give, 0)
        lax.fori_loop(0, chunks, take, 0)

    for chunk in range(chunks):
        far_copy(chunk).wait_recv()
        out_ref[:, chunk * CHUNK : (chunk + 1) * CHUNK] = (total[1, chunk] + summed[chunk]).astype(BF16)

    for chunk in range(chunks):
        far_copy(chunk).wait_send()
        for near in range(2):
            pair_copy(near, chunk).wait_send()

    @pl.when(has_after)
    def _():
        seg_copy.wait_send()

        def sent(head, carry):
            state_copy(head).wait_send()
            return carry

        lax.fori_loop(0, heads, sent, 0)


def finish(maps, adds, mapped, local_out, edges, gain, out_weight):
    heads, tok_local = mapped.shape[:2]
    width = out_weight.shape[1] // lax.axis_size("head")
    chunks = width // CHUNK
    dma = pltpu.SemaphoreType.DMA
    vmem = pl.BlockSpec(memory_space=pltpu.VMEM)
    return pl.pallas_call(
        finish_kernel,
        out_shape=jax.ShapeDtypeStruct((tok_local, width), BF16),
        in_specs=[vmem] * 6 + [pl.BlockSpec(memory_space=pl.ANY)],
        out_specs=vmem,
        scratch_shapes=[
            pltpu.VMEM(out_weight.shape, BF16),
            pltpu.VMEM((tok_local, heads * DV), BF16),
            pltpu.VMEM((heads, DK, DV), F32),
            pltpu.VMEM((heads, DK, DV), F32),
            pltpu.VMEM((8, 128), F32),
            pltpu.VMEM((2, chunks, tok_local, CHUNK), F32),
            pltpu.VMEM((2, chunks, tok_local, CHUNK), F32),
            pltpu.VMEM((2, chunks, tok_local, CHUNK), F32),
            pltpu.VMEM((chunks, tok_local, CHUNK), F32),
            dma,
            dma,
            dma,
            dma((heads,)),
            dma((heads,)),
            dma((2, chunks)),
            dma((2, chunks)),
            dma((chunks,)),
            dma((chunks,)),
        ],
        compiler_params=pltpu.CompilerParams(
            vmem_limit_bytes=48 * 1024 * 1024, collective_id=0, has_side_effects=True
        ),
        cost_estimate=pl.CostEstimate(flops=4 * 10**9, bytes_accessed=14 * 10**6, transcendentals=10**4),
        name="chain_and_project",
    )(maps, adds, mapped, local_out, edges, gain, out_weight)


def shards(queries, keys, values, betas, log_decay, segment, gain, out_weight):
    parts = local_parts(queries, keys, values, betas, log_decay, segment)
    return finish(*parts, gain.reshape(1, -1), out_weight)


def solution(mesh):
    return jax.shard_map(
        shards,
        mesh=mesh,
        in_specs=(
            P("ctx", "head"),
            P("ctx", None, "head"),
            P("ctx", None, "head"),
            P(None, "head", "ctx"),
            P("head", "ctx"),
            P("ctx"),
            P("head"),
            P("head", None),
        ),
        out_specs=P("ctx", "head"),
        check_vma=False,
    )
```

```python
import functools
import jax
import jax.numpy as jnp
from jax import lax
from jax.experimental import pallas as pl
from jax.experimental.pallas import tpu as pltpu
from jax.sharding import PartitionSpec as P

DK = 128
DV = 128
GROUP = 64
ROWS = 2 * GROUP
HEADS_STEP = 2
F32 = jnp.float32
BF16 = jnp.bfloat16


def halves(a):
    if a.dtype == BF16:
        return a, None
    hi = a.astype(BF16)
    return hi, (a - hi.astype(F32)).astype(BF16)


def one(a, b):
    return jnp.dot(a, b, preferred_element_type=F32)


def beside_halves(a):
    return jnp.concatenate(halves(a), axis=1)


def under(b):
    return jnp.concatenate([b, b], axis=0)


def folded(product):
    half = product.shape[1] // 2
    return product[:, :half] + product[:, half:]


def mul_sided(a_sided, b_sided):
    return folded(one(a_sided, under(b_sided)))


def mul_wide(a, b):
    a_hi, a_lo = halves(a)
    b_hi, b_lo = halves(b)
    return one(jnp.concatenate([a_hi, a_lo, a_hi], axis=1), jnp.concatenate([b_hi, b_hi, b_lo], axis=0))


def lower_rows(a, size):
    return jnp.concatenate(
        [a[at + size : at + 2 * size] for at in range(0, ROWS, 2 * size)], axis=0
    )


def spread_rows(a, size):
    zero = jnp.zeros((size, a.shape[1]), a.dtype)
    return jnp.concatenate(
        [part for at in range(0, ROWS // 2, size) for part in (zero, a[at : at + size])], axis=0
    )


def exact(a, b):
    return lax.dot_general(
        a, b, (((1,), (0,)), ((), ())), precision=lax.Precision.HIGHEST, preferred_element_type=F32
    )


def local_kernel(
    q_ref, k_ref, v_ref, beta_ref, log_ref, seg_ref, map_ref, add_ref, mapped_ref, local_ref, edge_ref
):
    step = pl.program_id(0)
    blocks = q_ref.shape[0] // GROUP
    row = lax.broadcasted_iota(jnp.int32, (ROWS, ROWS), 0)
    col = lax.broadcasted_iota(jnp.int32, (ROWS, ROWS), 1)
    row_tok = lax.broadcasted_iota(jnp.int32, (GROUP, ROWS), 0)
    col_tok = lax.broadcasted_iota(jnp.int32, (GROUP, ROWS), 1)
    eye = (row == col).astype(F32)
    summing = ((row < GROUP) & (row <= col // 2)).astype(F32)
    spreading = ((row < GROUP) & (row == col // 2)).astype(F32)
    weaving = jnp.where(
        row < GROUP, (col == 2 * row).astype(F32), (col == 2 * (row - GROUP) + 1).astype(F32)
    )
    units = [(which, block) for which in range(HEADS_STEP) for block in range(blocks)]
    segs = seg_ref[...].astype(F32)
    zero = jnp.zeros((1, GROUP), F32)
    log_rows, beta_rows, seg_rows = [], [], []
    for which, block in units:
        head, toks = step * HEADS_STEP + which, slice(block * GROUP, (block + 1) * GROUP)
        log_row = log_ref[pl.ds(head, 1), :]
        first, second = (beta_ref[j, pl.ds(head, 1), :] for j in range(2))
        log_rows.append(jnp.concatenate([log_row[:, toks], zero], axis=1))
        beta_rows.append(jnp.concatenate([first[:, toks], second[:, toks]], axis=1))
        seg_rows.append(jnp.concatenate([segs[:, toks], zero], axis=1))
    count = len(units)
    log_rows, beta_rows, seg_rows = (jnp.concatenate(r, axis=0) for r in (log_rows, beta_rows, seg_rows))
    cum_rows = exact(log_rows, summing)
    strength_rows = exact(beta_rows, weaving)
    doc_rows = exact(seg_rows, spreading)
    tok_rows = exact(log_rows, ((row < GROUP) & (row <= col)).astype(F32))
    columns = jnp.transpose(
        jnp.concatenate(
            [cum_rows, strength_rows, doc_rows, tok_rows, seg_rows]
            + [jnp.zeros((ROWS - 5 * count, ROWS), F32)],
            axis=0,
        )
    )

    prepared = []
    for at, (which, block) in enumerate(units):
        toks = slice(block * GROUP, (block + 1) * GROUP)
        cum_row, beta_row, seg_row = (r[at : at + 1] for r in (cum_rows, strength_rows, doc_rows))
        cum_col, beta_col, seg_col, cum_tok, seg_tok = (
            columns[:, k * count + at : k * count + at + 1] for k in range(5)
        )
        cum_tok, seg_tok = cum_tok[:GROUP], seg_tok[:GROUP]
        start = segs[:, 0:1] if block == 0 else segs[:, block * GROUP - 1 : block * GROUP]
        last_seg = segs[:, (block + 1) * GROUP - 1 : (block + 1) * GROUP]
        cum_last = cum_row[:, ROWS - 1 : ROWS]

        lanes = slice(which * DK, (which + 1) * DK)
        keys = k_ref[block * ROWS : (block + 1) * ROWS, lanes]
        query = q_ref[toks, lanes]
        keys_t = jnp.transpose(keys.astype(F32)).astype(BF16)
        both = one(jnp.concatenate([keys, query], axis=0), keys_t)
        gram, meets = both[:ROWS], both[ROWS:]
        diagonal = gram * eye
        inv_row = lax.rsqrt(jnp.sum(diagonal, axis=0, keepdims=True) + 1e-06)
        inv_col = lax.rsqrt(jnp.sum(diagonal, axis=1, keepdims=True) + 1e-06)
        query_f = query.astype(F32)
        inv_query = lax.rsqrt(jnp.sum(query_f * query_f, axis=1, keepdims=True) + 1e-06)
        lower = jnp.where(
            (seg_col == seg_row) & (row > col),
            (beta_col * inv_col) * jnp.exp(cum_col - cum_row) * (gram * inv_row),
            0.0,
        )
        scores = jnp.where(
            (seg_tok == seg_row) & (col_tok <= 2 * row_tok + 1),
            inv_query * jnp.exp(cum_tok - cum_row) * (meets * inv_row),
            0.0,
        )
        entry_row = jnp.where(seg_row == start, jnp.exp(cum_row), 0.0)
        entry_tok = jnp.where(seg_tok == start, jnp.exp(cum_tok), 0.0)
        tail_col = jnp.where(seg_col == last_seg, jnp.exp(cum_last - cum_col), 0.0)
        tail_entry = jnp.where(last_seg == start, jnp.exp(cum_last), 0.0)
        prepared.append(
            dict(
                keys=keys,
                keys_t=keys_t,
                lower=lower,
                scores=scores,
                value_scale=beta_row,
                key_scale=beta_row * entry_row * inv_row,
                tail=tail_col * inv_col,
                tail_entry=tail_entry,
                reach=(entry_tok * inv_query) * query_f,
            )
        )

    inverses = [eye - jnp.where(row // 2 == col // 2, p["lower"], 0.0) for p in prepared]
    size = 2
    while size < ROWS:
        below = (row // (2 * size) == col // (2 * size)) & (row // size > col // size)
        sided = [beside_halves(x) for x in inverses]
        masked = [beside_halves(jnp.where(below, p["lower"], 0.0)) for p in prepared]
        if size < 16:
            inner = [beside_halves(mul_sided(m, s)) for m, s in zip(masked, sided)]
            inverses = [x - mul_sided(s, i) for x, s, i in zip(inverses, sided, inner)]
        else:
            inner = [beside_halves(mul_sided(lower_rows(m, size), s)) for m, s in zip(masked, sided)]
            inner = [spread_rows(i, size) for i in inner]
            change = [mul_sided(lower_rows(s, size), i) for s, i in zip(sided, inner)]
            inverses = [x - spread_rows(c, size) for x, c in zip(inverses, change)]
        size *= 2

    solved = []
    for (which, block), p, x in zip(units, prepared, inverses):
        values = v_ref[block * ROWS : (block + 1) * ROWS, which * DV : (which + 1) * DV]
        key_mix = one(beside_halves(x * p["key_scale"]), under(p["keys"]))
        pseudo = one(beside_halves(x * p["value_scale"]), under(values))
        solved.append(jnp.concatenate([key_mix, pseudo], axis=1))
    reads = [mul_wide(p["scores"], s) for p, s in zip(prepared, solved)]
    moves = []
    for p, s in zip(prepared, solved):
        twice = jnp.concatenate([p["keys_t"], p["keys_t"]], axis=1)
        moves.append(one(twice, jnp.concatenate(halves(s * p["tail"]), axis=0)))
    running = [None] * HEADS_STEP
    for block in range(blocks):
        for which in range(HEADS_STEP):
            at = which * blocks + block
            p, toks = prepared[at], slice(block * GROUP, (block + 1) * GROUP)
            reach = p["reach"] - reads[at][:, :DK]
            block_map = p["tail_entry"] * eye - moves[at][:, :DK]
            if block == 0:
                mapped, local = reach, reads[at][:, DK:]
                running[which] = jnp.concatenate([block_map, moves[at][:, DK:]], axis=1)
            else:
                out = mul_wide(jnp.concatenate([reach, block_map], axis=0), running[which])
                mapped, local = out[:GROUP, :DK], out[:GROUP, DK:] + reads[at][:, DK:]
                running[which] = jnp.concatenate(
                    [out[GROUP:, :DK], out[GROUP:, DK:] + moves[at][:, DK:]], axis=1
                )
            mapped_ref[which, toks, :] = beside_halves(mapped)
            local_ref[which, toks, :] = local
    for which in range(HEADS_STEP):
        map_ref[which] = beside_halves(jnp.transpose(running[which][:, :DK]))
        add_ref[which] = jnp.transpose(running[which][:, DK:])
    segs = seg_ref[...].astype(F32)
    edge_ref[0] = jnp.broadcast_to(segs[:, 0:1], (8, 128))
    edge_ref[1] = jnp.broadcast_to(segs[:, segs.shape[1] - 1 :], (8, 128))


def local_parts(queries, keys, values, betas, log_decay, segment):
    tok_local = queries.shape[0]
    heads_local = betas.shape[1]
    lanes = HEADS_STEP * DK
    whole = lambda *shape: pl.BlockSpec(shape, lambda h: (0,) * len(shape))
    per_head = lambda rows, width: pl.BlockSpec((HEADS_STEP, rows, width), lambda h: (h, 0, 0))
    shape = lambda rows, width, dtype: jax.ShapeDtypeStruct((heads_local, rows, width), dtype)
    return pl.pallas_call(
        local_kernel,
        grid=(heads_local // HEADS_STEP,),
        in_specs=[
            pl.BlockSpec((tok_local, lanes), lambda h: (0, h)),
            pl.BlockSpec((2 * tok_local, lanes), lambda h: (0, h)),
            pl.BlockSpec((2 * tok_local, lanes), lambda h: (0, h)),
            whole(2, heads_local, tok_local),
            whole(heads_local, tok_local),
            whole(1, tok_local),
        ],
        out_specs=[
            per_head(DK, 2 * DK),
            per_head(DV, DK),
            per_head(tok_local, 2 * DK),
            per_head(tok_local, DV),
            whole(2, 8, 128),
        ],
        out_shape=[
            shape(DK, 2 * DK, BF16),
            shape(DV, DK, F32),
            shape(tok_local, 2 * DK, BF16),
            shape(tok_local, DV, F32),
            jax.ShapeDtypeStruct((2, 8, 128), F32),
        ],
        compiler_params=pltpu.CompilerParams(vmem_limit_bytes=60 * 1024 * 1024),
        cost_estimate=pl.CostEstimate(flops=12 * 10**9, bytes_accessed=8 * 10**6, transcendentals=10**6),
        name="local_blocks",
    )(
        queries,
        keys.reshape(2 * tok_local, -1),
        values.reshape(2 * tok_local, -1),
        betas,
        log_decay,
        segment.reshape(1, tok_local),
    )


MESH = pl.DeviceIdType.MESH
CHUNK = 256
PIECES = 2


def finish_kernel(
    map_ref, add_ref, mapped_ref, local_ref, edge_ref, gain_ref, weight_ref, out_ref,
    weight, normed, states, leaving, seg_in, outgoing, incoming, total, summed,
    weight_sem, seg_send, seg_recv, chain_send, chain_recv, pair_send, pair_recv, far_send, far_recv,
):
    place, places = lax.axis_index("ctx"), lax.axis_size("ctx")
    mine = lax.axis_index("head")
    heads = map_ref.shape[0]
    width = out_ref.shape[1]
    chunks = width // CHUNK
    rows = DV // PIECES
    beside = mine + 1 - 2 * lax.rem(mine, 2)
    across = lax.rem(mine + 2, 4)
    diagonal = 3 - mine
    after, before = place + 1, place - 1
    has_after, has_before = place < places - 1, place > 0

    fetch = pltpu.make_async_copy(weight_ref, weight, weight_sem)
    fetch.start()
    barrier = pltpu.get_barrier_semaphore()
    for partner in (beside, across):
        pl.semaphore_signal(barrier, inc=1, device_id=(place, partner), device_id_type=MESH)

    @pl.when(has_after)
    def _():
        pl.semaphore_signal(barrier, inc=1, device_id=(after, mine), device_id_type=MESH)

    @pl.when(has_before)
    def _():
        pl.semaphore_signal(barrier, inc=1, device_id=(before, mine), device_id_type=MESH)

    pl.semaphore_wait(barrier, 2 + has_after.astype(jnp.int32) + has_before.astype(jnp.int32))

    seg_copy = pltpu.make_async_remote_copy(
        src_ref=edge_ref.at[1], dst_ref=seg_in, send_sem=seg_send, recv_sem=seg_recv,
        device_id=(after, mine), device_id_type=MESH,
    )

    def state_copy(head, piece):
        return pltpu.make_async_remote_copy(
            src_ref=leaving.at[head, piece], dst_ref=states.at[head, piece],
            send_sem=chain_send.at[head, piece], recv_sem=chain_recv.at[head, piece],
            device_id=(after, mine), device_id_type=MESH,
        )

    def attend(head, state):
        attended = local_ref[head]
        if state is not None:
            attended = attended + mul_sided(mapped_ref[head], beside_halves(jnp.transpose(state)))
        inverse_rms = 1.0 / jnp.sqrt(jnp.mean(attended * attended, axis=-1, keepdims=True) + 1e-06)
        lanes = pl.ds(pl.multiple_of(head * DV, DV), DV)
        normed[:, lanes] = (attended * inverse_rms * gain_ref[:, lanes]).astype(BF16)

    @pl.when(place == 0)
    def _():
        seg_copy.start()

        def first(head, carry):
            for piece in range(PIECES):
                leaving[head, piece] = add_ref[head, piece * rows : (piece + 1) * rows, :]
                state_copy(head, piece).start()
            return carry

        lax.fori_loop(0, heads, first, 0)

        def read(head, carry):
            attend(head, None)
            return carry

        lax.fori_loop(0, heads, read, 0)

    @pl.when(has_before)
    def _():
        @pl.when(has_after)
        def _():
            seg_copy.start()

        seg_copy.wait_recv()
        linked = seg_in[0:1, :] == edge_ref[0, 0:1, :]

        def link(head, carry):
            carried = map_ref[head]
            whole = []
            for piece in range(PIECES):
                added = add_ref[head, piece * rows : (piece + 1) * rows, :]
                state_copy(head, piece).wait_recv()
                state = jnp.where(linked, states[head, piece], 0.0)
                whole.append(state)

                @pl.when(has_after)
                def _():
                    leaving[head, piece] = mul_sided(beside_halves(state), carried) + added
                    state_copy(head, piece).start()

            attend(head, jnp.concatenate(whole, axis=0))
            return carry

        lax.fori_loop(0, heads, link, 0)

    fetch.wait()

    def product(owner, chunk):
        lanes = pl.ds(pl.multiple_of(owner * width + chunk * CHUNK, CHUNK), CHUNK)
        return one(normed[...], weight[:, lanes])

    def pair_copy(near, chunk):
        return pltpu.make_async_remote_copy(
            src_ref=outgoing.at[near, chunk], dst_ref=incoming.at[near, chunk],
            send_sem=pair_send.at[near, chunk], recv_sem=pair_recv.at[near, chunk],
            device_id=(place, beside), device_id_type=MESH,
        )

    def far_copy(chunk):
        return pltpu.make_async_remote_copy(
            src_ref=total.at[0, chunk], dst_ref=summed.at[chunk],
            send_sem=far_send.at[chunk], recv_sem=far_recv.at[chunk],
            device_id=(place, across), device_id_type=MESH,
        )

    for near, theirs, ours in ((0, diagonal, across), (1, beside, mine)):

        def give(chunk, carry):
            outgoing[near, chunk] = product(theirs, chunk)
            pair_copy(near, chunk).start()
            return carry

        def take(chunk, carry):
            part = product(ours, chunk)
            pair_copy(near, chunk).wait_recv()
            total[near, chunk] = part + incoming[near, chunk]
            if near == 0:
                far_copy(chunk).start()
            return carry

        lax.fori_loop(0, chunks, give, 0)
        lax.fori_loop(0, chunks, take, 0)

    for chunk in range(chunks):
        far_copy(chunk).wait_recv()
        out_ref[:, chunk * CHUNK : (chunk + 1) * CHUNK] = (total[1, chunk] + summed[chunk]).astype(BF16)

    for chunk in range(chunks):
        far_copy(chunk).wait_send()
        for near in range(2):
            pair_copy(near, chunk).wait_send()

    @pl.when(has_after)
    def _():
        seg_copy.wait_send()

        def sent(head, carry):
            for piece in range(PIECES):
                state_copy(head, piece).wait_send()
            return carry

        lax.fori_loop(0, heads, sent, 0)


def finish(maps, adds, mapped, local_out, edges, gain, out_weight):
    heads, tok_local = mapped.shape[:2]
    width = out_weight.shape[1] // lax.axis_size("head")
    chunks = width // CHUNK
    dma = pltpu.SemaphoreType.DMA
    vmem = pl.BlockSpec(memory_space=pltpu.VMEM)
    return pl.pallas_call(
        finish_kernel,
        out_shape=jax.ShapeDtypeStruct((tok_local, width), BF16),
        in_specs=[vmem] * 6 + [pl.BlockSpec(memory_space=pl.ANY)],
        out_specs=vmem,
        scratch_shapes=[
            pltpu.VMEM(out_weight.shape, BF16),
            pltpu.VMEM((tok_local, heads * DV), BF16),
            pltpu.VMEM((heads, PIECES, DV // PIECES, DK), F32),
            pltpu.VMEM((heads, PIECES, DV // PIECES, DK), F32),
            pltpu.VMEM((8, 128), F32),
            pltpu.VMEM((2, chunks, tok_local, CHUNK), F32),
            pltpu.VMEM((2, chunks, tok_local, CHUNK), F32),
            pltpu.VMEM((2, chunks, tok_local, CHUNK), F32),
            pltpu.VMEM((chunks, tok_local, CHUNK), F32),
            dma,
            dma,
            dma,
            dma((heads, PIECES)),
            dma((heads, PIECES)),
            dma((2, chunks)),
            dma((2, chunks)),
            dma((chunks,)),
            dma((chunks,)),
        ],
        compiler_params=pltpu.CompilerParams(
            vmem_limit_bytes=60 * 1024 * 1024, collective_id=0, has_side_effects=True
        ),
        cost_estimate=pl.CostEstimate(flops=4 * 10**9, bytes_accessed=14 * 10**6, transcendentals=10**4),
        name="chain_and_project",
    )(maps, adds, mapped, local_out, edges, gain, out_weight)


def shards(queries, keys, values, betas, log_decay, segment, gain, out_weight):
    parts = local_parts(queries, keys, values, betas, log_decay, segment)
    return finish(*parts, gain.reshape(1, -1), out_weight)


def solution(mesh):
    return jax.shard_map(
        shards,
        mesh=mesh,
        in_specs=(
            P("ctx", "head"),
            P("ctx", None, "head"),
            P("ctx", None, "head"),
            P(None, "head", "ctx"),
            P("head", "ctx"),
            P("ctx"),
            P("head"),
            P("head", None),
        ),
        out_specs=P("ctx", "head"),
        check_vma=False,
    )
```

```python
import functools
import jax
import jax.numpy as jnp
from jax import lax
from jax.experimental import pallas as pl
from jax.experimental.pallas import tpu as pltpu
from jax.sharding import PartitionSpec as P

DK = 128
DV = 128
GROUP = 64
ROWS = 2 * GROUP
HEADS_STEP = 2
REFINES = 1
F32 = jnp.float32
BF16 = jnp.bfloat16


def halves(a):
    if a.dtype == BF16:
        return a, None
    hi = a.astype(BF16)
    return hi, (a - hi.astype(F32)).astype(BF16)


def one(a, b):
    return jnp.dot(a, b, preferred_element_type=F32)


def beside_halves(a):
    return jnp.concatenate(halves(a), axis=1)


def under(b):
    return jnp.concatenate([b, b], axis=0)


def folded(product):
    half = product.shape[1] // 2
    return product[:, :half] + product[:, half:]


def mul_sided(a_sided, b_sided):
    return folded(one(a_sided, under(b_sided)))


def mul_wide(a, b):
    a_hi, a_lo = halves(a)
    b_hi, b_lo = halves(b)
    both = one(jnp.concatenate([a_hi, a_lo], axis=0), b_hi)
    return both[: a.shape[0]] + both[a.shape[0] :] + one(a_hi, b_lo)


def lower_rows(a, size):
    return jnp.concatenate(
        [a[at + size : at + 2 * size] for at in range(0, ROWS, 2 * size)], axis=0
    )


def spread_rows(a, size):
    zero = jnp.zeros((size, a.shape[1]), a.dtype)
    return jnp.concatenate(
        [part for at in range(0, ROWS // 2, size) for part in (zero, a[at : at + size])], axis=0
    )


def exact(a, b):
    return lax.dot_general(
        a, b, (((1,), (0,)), ((), ())), precision=lax.Precision.HIGHEST, preferred_element_type=F32
    )


def local_kernel(
    q_ref, k_ref, v_ref, beta_ref, log_ref, seg_ref, map_ref, add_ref, mapped_ref, local_ref, edge_ref
):
    step = pl.program_id(0)
    blocks = q_ref.shape[0] // GROUP
    row = lax.broadcasted_iota(jnp.int32, (ROWS, ROWS), 0)
    col = lax.broadcasted_iota(jnp.int32, (ROWS, ROWS), 1)
    row_tok = lax.broadcasted_iota(jnp.int32, (GROUP, ROWS), 0)
    col_tok = lax.broadcasted_iota(jnp.int32, (GROUP, ROWS), 1)
    eye = (row == col).astype(F32)
    summing = ((row < GROUP) & (row <= col // 2)).astype(F32)
    spreading = ((row < GROUP) & (row == col // 2)).astype(F32)
    weaving = jnp.where(
        row < GROUP, (col == 2 * row).astype(F32), (col == 2 * (row - GROUP) + 1).astype(F32)
    )
    units = [(which, block) for which in range(HEADS_STEP) for block in range(blocks)]
    segs = seg_ref[...].astype(F32)
    zero = jnp.zeros((1, GROUP), F32)
    log_rows, beta_rows, seg_rows = [], [], []
    for which, block in units:
        head, toks = step * HEADS_STEP + which, slice(block * GROUP, (block + 1) * GROUP)
        log_row = log_ref[pl.ds(head, 1), :]
        first, second = (beta_ref[j, pl.ds(head, 1), :] for j in range(2))
        log_rows.append(jnp.concatenate([log_row[:, toks], zero], axis=1))
        beta_rows.append(jnp.concatenate([first[:, toks], second[:, toks]], axis=1))
        seg_rows.append(jnp.concatenate([segs[:, toks], zero], axis=1))
    count = len(units)
    log_rows, beta_rows, seg_rows = (jnp.concatenate(r, axis=0) for r in (log_rows, beta_rows, seg_rows))
    cum_rows = exact(log_rows, summing)
    strength_rows = exact(beta_rows, weaving)
    doc_rows = exact(seg_rows, spreading)
    tok_rows = exact(log_rows, ((row < GROUP) & (row <= col)).astype(F32))
    columns = jnp.transpose(
        jnp.concatenate(
            [cum_rows, strength_rows, doc_rows, tok_rows, seg_rows]
            + [jnp.zeros((ROWS - 5 * count, ROWS), F32)],
            axis=0,
        )
    )

    prepared = []
    for at, (which, block) in enumerate(units):
        toks = slice(block * GROUP, (block + 1) * GROUP)
        cum_row, beta_row, seg_row = (r[at : at + 1] for r in (cum_rows, strength_rows, doc_rows))
        cum_col, beta_col, seg_col, cum_tok, seg_tok = (
            columns[:, k * count + at : k * count + at + 1] for k in range(5)
        )
        cum_tok, seg_tok = cum_tok[:GROUP], seg_tok[:GROUP]
        start = segs[:, 0:1] if block == 0 else segs[:, block * GROUP - 1 : block * GROUP]
        last_seg = segs[:, (block + 1) * GROUP - 1 : (block + 1) * GROUP]
        cum_last = cum_row[:, ROWS - 1 : ROWS]

        lanes = slice(which * DK, (which + 1) * DK)
        keys = k_ref[block * ROWS : (block + 1) * ROWS, lanes]
        query = q_ref[toks, lanes]
        keys_t = jnp.transpose(keys.astype(F32)).astype(BF16)
        both = one(jnp.concatenate([keys, query], axis=0), keys_t)
        gram, meets = both[:ROWS], both[ROWS:]
        diagonal = gram * eye
        inv_row = lax.rsqrt(jnp.sum(diagonal, axis=0, keepdims=True) + 1e-06)
        inv_col = lax.rsqrt(jnp.sum(diagonal, axis=1, keepdims=True) + 1e-06)
        query_f = query.astype(F32)
        inv_query = lax.rsqrt(jnp.sum(query_f * query_f, axis=1, keepdims=True) + 1e-06)
        lower = jnp.where(
            (seg_col == seg_row) & (row > col),
            (beta_col * inv_col) * jnp.exp(cum_col - cum_row) * (gram * inv_row),
            0.0,
        )
        scores = jnp.where(
            (seg_tok == seg_row) & (col_tok <= 2 * row_tok + 1),
            inv_query * jnp.exp(cum_tok - cum_row) * (meets * inv_row),
            0.0,
        )
        entry_row = jnp.where(seg_row == start, jnp.exp(cum_row), 0.0)
        entry_tok = jnp.where(seg_tok == start, jnp.exp(cum_tok), 0.0)
        tail_col = jnp.where(seg_col == last_seg, jnp.exp(cum_last - cum_col), 0.0)
        tail_entry = jnp.where(last_seg == start, jnp.exp(cum_last), 0.0)
        prepared.append(
            dict(
                keys=keys,
                keys_t=keys_t,
                lower=lower,
                scores=scores,
                value_scale=beta_row,
                key_scale=beta_row * entry_row * inv_row,
                tail=tail_col * inv_col,
                tail_entry=tail_entry,
                reach=(entry_tok * inv_query) * query_f,
            )
        )

    inverses = [eye - jnp.where(row // 2 == col // 2, p["lower"], 0.0) for p in prepared]
    size = 2
    lowers = [p["lower"].astype(BF16) for p in prepared]
    nothing = jnp.zeros((ROWS, ROWS), BF16)
    while size < ROWS:
        below = (row // (2 * size) == col // (2 * size)) & (row // size > col // size)
        rounded = [x.astype(BF16) for x in inverses]
        masked = [jnp.where(below, low, nothing) for low in lowers]
        if size < 16:
            inner = [one(m, x).astype(BF16) for m, x in zip(masked, rounded)]
            inverses = [x - one(r, i) for x, r, i in zip(inverses, rounded, inner)]
        else:
            inner = [one(lower_rows(m, size), x).astype(BF16) for m, x in zip(masked, rounded)]
            inner = [spread_rows(i, size) for i in inner]
            change = [one(lower_rows(r, size), i) for r, i in zip(rounded, inner)]
            inverses = [x - spread_rows(c, size) for x, c in zip(inverses, change)]
        size *= 2
    for _ in range(REFINES):
        sided = [beside_halves(x) for x in inverses]
        off = [eye - x - mul_sided(beside_halves(p["lower"]), s) for x, p, s in zip(inverses, prepared, sided)]
        inverses = [x + one(s[:, :ROWS], o.astype(BF16)) for x, s, o in zip(inverses, sided, off)]

    solved = []
    for (which, block), p, x in zip(units, prepared, inverses):
        values = v_ref[block * ROWS : (block + 1) * ROWS, which * DV : (which + 1) * DV]
        key_mix = one(beside_halves(x * p["key_scale"]), under(p["keys"]))
        pseudo = one(beside_halves(x * p["value_scale"]), under(values))
        solved.append(jnp.concatenate([key_mix, pseudo], axis=1))
    reads = []
    for p, s in zip(prepared, solved):
        s_hi, s_lo = halves(s)
        score_hi, score_lo = halves(p["scores"])
        both = one(jnp.concatenate([score_hi, score_lo], axis=0), s_hi)
        reads.append(both[:GROUP] + both[GROUP:] + one(score_hi, s_lo))
    moves = []
    for p, s in zip(prepared, solved):
        twice = jnp.concatenate([p["keys_t"], p["keys_t"]], axis=1)
        moves.append(one(twice, jnp.concatenate(halves(s * p["tail"]), axis=0)))
    running = [None] * HEADS_STEP
    for block in range(blocks):
        for which in range(HEADS_STEP):
            at = which * blocks + block
            p, toks = prepared[at], slice(block * GROUP, (block + 1) * GROUP)
            reach = p["reach"] - reads[at][:, :DK]
            block_map = p["tail_entry"] * eye - moves[at][:, :DK]
            if block == 0:
                mapped, local = reach, reads[at][:, DK:]
                running[which] = jnp.concatenate([block_map, moves[at][:, DK:]], axis=1)
            else:
                out = mul_wide(jnp.concatenate([reach, block_map], axis=0), running[which])
                mapped, local = out[:GROUP, :DK], out[:GROUP, DK:] + reads[at][:, DK:]
                running[which] = jnp.concatenate(
                    [out[GROUP:, :DK], out[GROUP:, DK:] + moves[at][:, DK:]], axis=1
                )
            mapped_ref[which, toks, :] = beside_halves(mapped)
            local_ref[which, toks, :] = local
    for which in range(HEADS_STEP):
        map_ref[which] = beside_halves(jnp.transpose(running[which][:, :DK]))
        add_ref[which] = jnp.transpose(running[which][:, DK:])
    segs = seg_ref[...].astype(F32)
    edge_ref[0] = jnp.broadcast_to(segs[:, 0:1], (8, 128))
    edge_ref[1] = jnp.broadcast_to(segs[:, segs.shape[1] - 1 :], (8, 128))


def local_parts(queries, keys, values, betas, log_decay, segment):
    tok_local = queries.shape[0]
    heads_local = betas.shape[1]
    lanes = HEADS_STEP * DK
    whole = lambda *shape: pl.BlockSpec(shape, lambda h: (0,) * len(shape))
    per_head = lambda rows, width: pl.BlockSpec((HEADS_STEP, rows, width), lambda h: (h, 0, 0))
    shape = lambda rows, width, dtype: jax.ShapeDtypeStruct((heads_local, rows, width), dtype)
    return pl.pallas_call(
        local_kernel,
        grid=(heads_local // HEADS_STEP,),
        in_specs=[
            pl.BlockSpec((tok_local, lanes), lambda h: (0, h)),
            pl.BlockSpec((2 * tok_local, lanes), lambda h: (0, h)),
            pl.BlockSpec((2 * tok_local, lanes), lambda h: (0, h)),
            whole(2, heads_local, tok_local),
            whole(heads_local, tok_local),
            whole(1, tok_local),
        ],
        out_specs=[
            per_head(DK, 2 * DK),
            per_head(DV, DK),
            per_head(tok_local, 2 * DK),
            per_head(tok_local, DV),
            whole(2, 8, 128),
        ],
        out_shape=[
            shape(DK, 2 * DK, BF16),
            shape(DV, DK, F32),
            shape(tok_local, 2 * DK, BF16),
            shape(tok_local, DV, F32),
            jax.ShapeDtypeStruct((2, 8, 128), F32),
        ],
        compiler_params=pltpu.CompilerParams(vmem_limit_bytes=60 * 1024 * 1024),
        cost_estimate=pl.CostEstimate(flops=12 * 10**9, bytes_accessed=8 * 10**6, transcendentals=10**6),
        name="local_blocks",
    )(
        queries,
        keys.reshape(2 * tok_local, -1),
        values.reshape(2 * tok_local, -1),
        betas,
        log_decay,
        segment.reshape(1, tok_local),
    )


MESH = pl.DeviceIdType.MESH
CHUNK = 256
PIECES = 2


def finish_kernel(
    map_ref, add_ref, mapped_ref, local_ref, edge_ref, gain_ref, weight_ref, out_ref,
    weight, normed, states, leaving, seg_in, outgoing, incoming, total, summed,
    weight_sem, seg_send, seg_recv, chain_send, chain_recv, pair_send, pair_recv, far_send, far_recv,
):
    place, places = lax.axis_index("ctx"), lax.axis_size("ctx")
    mine = lax.axis_index("head")
    heads = map_ref.shape[0]
    width = out_ref.shape[1]
    chunks = width // CHUNK
    rows = DV // PIECES
    beside = mine + 1 - 2 * lax.rem(mine, 2)
    across = lax.rem(mine + 2, 4)
    diagonal = 3 - mine
    after, before = place + 1, place - 1
    has_after, has_before = place < places - 1, place > 0

    fetch = pltpu.make_async_copy(weight_ref, weight, weight_sem)
    fetch.start()
    barrier = pltpu.get_barrier_semaphore()
    for partner in (beside, across):
        pl.semaphore_signal(barrier, inc=1, device_id=(place, partner), device_id_type=MESH)

    @pl.when(has_after)
    def _():
        pl.semaphore_signal(barrier, inc=1, device_id=(after, mine), device_id_type=MESH)

    @pl.when(has_before)
    def _():
        pl.semaphore_signal(barrier, inc=1, device_id=(before, mine), device_id_type=MESH)

    pl.semaphore_wait(barrier, 2 + has_after.astype(jnp.int32) + has_before.astype(jnp.int32))

    seg_copy = pltpu.make_async_remote_copy(
        src_ref=edge_ref.at[1], dst_ref=seg_in, send_sem=seg_send, recv_sem=seg_recv,
        device_id=(after, mine), device_id_type=MESH,
    )

    def state_copy(head, piece):
        return pltpu.make_async_remote_copy(
            src_ref=leaving.at[head, piece], dst_ref=states.at[head, piece],
            send_sem=chain_send.at[head, piece], recv_sem=chain_recv.at[head, piece],
            device_id=(after, mine), device_id_type=MESH,
        )

    def attend(head, state):
        attended = local_ref[head]
        if state is not None:
            attended = attended + mul_sided(mapped_ref[head], beside_halves(jnp.transpose(state)))
        inverse_rms = 1.0 / jnp.sqrt(jnp.mean(attended * attended, axis=-1, keepdims=True) + 1e-06)
        lanes = pl.ds(pl.multiple_of(head * DV, DV), DV)
        normed[:, lanes] = (attended * inverse_rms * gain_ref[:, lanes]).astype(BF16)

    @pl.when(place == 0)
    def _():
        seg_copy.start()

        def first(head, carry):
            for piece in range(PIECES):
                leaving[head, piece] = add_ref[head, piece * rows : (piece + 1) * rows, :]
                state_copy(head, piece).start()
            return carry

        lax.fori_loop(0, heads, first, 0)

        def read(head, carry):
            attend(head, None)
            return carry

        lax.fori_loop(0, heads, read, 0)

    @pl.when(has_before)
    def _():
        @pl.when(has_after)
        def _():
            seg_copy.start()

        seg_copy.wait_recv()
        linked = seg_in[0:1, :] == edge_ref[0, 0:1, :]

        def link(head, carry):
            carried = map_ref[head]
            whole = []
            for piece in range(PIECES):
                added = add_ref[head, piece * rows : (piece + 1) * rows, :]
                state_copy(head, piece).wait_recv()
                state = jnp.where(linked, states[head, piece], 0.0)
                whole.append(state)

                @pl.when(has_after)
                def _():
                    leaving[head, piece] = mul_sided(beside_halves(state), carried) + added
                    state_copy(head, piece).start()

            attend(head, jnp.concatenate(whole, axis=0))
            return carry

        lax.fori_loop(0, heads, link, 0)

    fetch.wait()

    def product(owner, chunk):
        lanes = pl.ds(pl.multiple_of(owner * width + chunk * CHUNK, CHUNK), CHUNK)
        return one(normed[...], weight[:, lanes])

    def pair_copy(near, chunk):
        return pltpu.make_async_remote_copy(
            src_ref=outgoing.at[near, chunk], dst_ref=incoming.at[near, chunk],
            send_sem=pair_send.at[near, chunk], recv_sem=pair_recv.at[near, chunk],
            device_id=(place, beside), device_id_type=MESH,
        )

    def far_copy(chunk):
        return pltpu.make_async_remote_copy(
            src_ref=total.at[0, chunk], dst_ref=summed.at[chunk],
            send_sem=far_send.at[chunk], recv_sem=far_recv.at[chunk],
            device_id=(place, across), device_id_type=MESH,
        )

    for near, theirs, ours in ((0, diagonal, across), (1, beside, mine)):

        def give(chunk, carry):
            outgoing[near, chunk] = product(theirs, chunk)
            pair_copy(near, chunk).start()
            return carry

        def take(chunk, carry):
            part = product(ours, chunk)
            pair_copy(near, chunk).wait_recv()
            total[near, chunk] = part + incoming[near, chunk]
            if near == 0:
                far_copy(chunk).start()
            return carry

        lax.fori_loop(0, chunks, give, 0)
        lax.fori_loop(0, chunks, take, 0)

    for chunk in range(chunks):
        far_copy(chunk).wait_recv()
        out_ref[:, chunk * CHUNK : (chunk + 1) * CHUNK] = (total[1, chunk] + summed[chunk]).astype(BF16)

    for chunk in range(chunks):
        far_copy(chunk).wait_send()
        for near in range(2):
            pair_copy(near, chunk).wait_send()

    @pl.when(has_after)
    def _():
        seg_copy.wait_send()

        def sent(head, carry):
            for piece in range(PIECES):
                state_copy(head, piece).wait_send()
            return carry

        lax.fori_loop(0, heads, sent, 0)


def finish(maps, adds, mapped, local_out, edges, gain, out_weight):
    heads, tok_local = mapped.shape[:2]
    width = out_weight.shape[1] // lax.axis_size("head")
    chunks = width // CHUNK
    dma = pltpu.SemaphoreType.DMA
    vmem = pl.BlockSpec(memory_space=pltpu.VMEM)
    return pl.pallas_call(
        finish_kernel,
        out_shape=jax.ShapeDtypeStruct((tok_local, width), BF16),
        in_specs=[vmem] * 6 + [pl.BlockSpec(memory_space=pl.ANY)],
        out_specs=vmem,
        scratch_shapes=[
            pltpu.VMEM(out_weight.shape, BF16),
            pltpu.VMEM((tok_local, heads * DV), BF16),
            pltpu.VMEM((heads, PIECES, DV // PIECES, DK), F32),
            pltpu.VMEM((heads, PIECES, DV // PIECES, DK), F32),
            pltpu.VMEM((8, 128), F32),
            pltpu.VMEM((2, chunks, tok_local, CHUNK), F32),
            pltpu.VMEM((2, chunks, tok_local, CHUNK), F32),
            pltpu.VMEM((2, chunks, tok_local, CHUNK), F32),
            pltpu.VMEM((chunks, tok_local, CHUNK), F32),
            dma,
            dma,
            dma,
            dma((heads, PIECES)),
            dma((heads, PIECES)),
            dma((2, chunks)),
            dma((2, chunks)),
            dma((chunks,)),
            dma((chunks,)),
        ],
        compiler_params=pltpu.CompilerParams(
            vmem_limit_bytes=48 * 1024 * 1024, collective_id=0, has_side_effects=True
        ),
        cost_estimate=pl.CostEstimate(flops=4 * 10**9, bytes_accessed=14 * 10**6, transcendentals=10**4),
        name="chain_and_project",
    )(maps, adds, mapped, local_out, edges, gain, out_weight)


def shards(queries, keys, values, betas, log_decay, segment, gain, out_weight):
    parts = local_parts(queries, keys, values, betas, log_decay, segment)
    return finish(*parts, gain.reshape(1, -1), out_weight)


def solution(mesh):
    return jax.shard_map(
        shards,
        mesh=mesh,
        in_specs=(
            P("ctx", "head"),
            P("ctx", None, "head"),
            P("ctx", None, "head"),
            P(None, "head", "ctx"),
            P("head", "ctx"),
            P("ctx"),
            P("head"),
            P("head", None),
        ),
        out_specs=P("ctx", "head"),
        check_vma=False,
    )
```

```python
import functools
import jax
import jax.numpy as jnp
from jax import lax
from jax.experimental import pallas as pl
from jax.experimental.pallas import tpu as pltpu
from jax.sharding import PartitionSpec as P

DK = 128
DV = 128
GROUP = 64
ROWS = 2 * GROUP
HEADS_STEP = 4
REFINES = 2
F32 = jnp.float32
BF16 = jnp.bfloat16


def halves(a):
    if a.dtype == BF16:
        return a, None
    hi = a.astype(BF16)
    return hi, (a - hi.astype(F32)).astype(BF16)


def one(a, b):
    return jnp.dot(a, b, preferred_element_type=F32)


def beside_halves(a):
    return jnp.concatenate(halves(a), axis=1)


def under(b):
    return jnp.concatenate([b, b], axis=0)


def folded(product):
    half = product.shape[1] // 2
    return product[:, :half] + product[:, half:]


def mul_sided(a_sided, b_sided):
    return folded(one(a_sided, under(b_sided)))


def mul_wide(a, b):
    a_hi, a_lo = halves(a)
    b_hi, b_lo = halves(b)
    both = one(jnp.concatenate([a_hi, a_lo], axis=0), b_hi)
    return both[: a.shape[0]] + both[a.shape[0] :] + one(a_hi, b_lo)


def lower_rows(a, size):
    return jnp.concatenate(
        [a[at + size : at + 2 * size] for at in range(0, ROWS, 2 * size)], axis=0
    )


def spread_rows(a, size):
    zero = jnp.zeros((size, a.shape[1]), a.dtype)
    return jnp.concatenate(
        [part for at in range(0, ROWS // 2, size) for part in (zero, a[at : at + size])], axis=0
    )


def exact(a, b):
    return lax.dot_general(
        a, b, (((1,), (0,)), ((), ())), precision=lax.Precision.HIGHEST, preferred_element_type=F32
    )


def local_kernel(
    q_ref, k_ref, v_ref, beta_ref, log_ref, seg_ref, map_ref, add_ref, mapped_ref, local_ref, edge_ref
):
    step = pl.program_id(0)
    blocks = q_ref.shape[0] // GROUP
    row = lax.broadcasted_iota(jnp.int32, (ROWS, ROWS), 0)
    col = lax.broadcasted_iota(jnp.int32, (ROWS, ROWS), 1)
    row_tok = lax.broadcasted_iota(jnp.int32, (GROUP, ROWS), 0)
    col_tok = lax.broadcasted_iota(jnp.int32, (GROUP, ROWS), 1)
    eye = (row == col).astype(F32)
    apart = row ^ col
    half_col = col >> 1
    summing = ((row < GROUP) & (row <= half_col)).astype(F32)
    spreading = ((row < GROUP) & (row == half_col)).astype(F32)
    weaving = jnp.where(
        row < GROUP, (col == 2 * row).astype(F32), (col == 2 * (row - GROUP) + 1).astype(F32)
    )
    units = [(which, block) for which in range(HEADS_STEP) for block in range(blocks)]
    segs = seg_ref[...].astype(F32)
    zero = jnp.zeros((1, GROUP), F32)
    log_rows, beta_rows, seg_rows = [], [], []
    for which, block in units:
        head, toks = step * HEADS_STEP + which, slice(block * GROUP, (block + 1) * GROUP)
        log_row = log_ref[pl.ds(head, 1), :]
        first, second = (beta_ref[j, pl.ds(head, 1), :] for j in range(2))
        log_rows.append(jnp.concatenate([log_row[:, toks], zero], axis=1))
        beta_rows.append(jnp.concatenate([first[:, toks], second[:, toks]], axis=1))
        seg_rows.append(jnp.concatenate([segs[:, toks], zero], axis=1))
    count = len(units)
    log_rows, beta_rows, seg_rows = (jnp.concatenate(r, axis=0) for r in (log_rows, beta_rows, seg_rows))
    cum_rows = exact(log_rows, summing)
    strength_rows = exact(beta_rows, weaving)
    doc_rows = exact(seg_rows, spreading)
    tok_rows = exact(log_rows, ((row < GROUP) & (row <= col)).astype(F32))
    columns = jnp.transpose(
        jnp.concatenate(
            [cum_rows, strength_rows, doc_rows, tok_rows, seg_rows]
            + [jnp.zeros((ROWS - 5 * count, ROWS), F32)],
            axis=0,
        )
    )

    prepared = []
    for at, (which, block) in enumerate(units):
        toks = slice(block * GROUP, (block + 1) * GROUP)
        cum_row, beta_row, seg_row = (r[at : at + 1] for r in (cum_rows, strength_rows, doc_rows))
        cum_col, beta_col, seg_col, cum_tok, seg_tok = (
            columns[:, k * count + at : k * count + at + 1] for k in range(5)
        )
        cum_tok, seg_tok = cum_tok[:GROUP], seg_tok[:GROUP]
        start = segs[:, 0:1] if block == 0 else segs[:, block * GROUP - 1 : block * GROUP]
        last_seg = segs[:, (block + 1) * GROUP - 1 : (block + 1) * GROUP]
        cum_last = cum_row[:, ROWS - 1 : ROWS]

        lanes = slice(which * DK, (which + 1) * DK)
        keys = k_ref[block * ROWS : (block + 1) * ROWS, lanes]
        query = q_ref[toks, lanes]
        keys_t = jnp.transpose(keys.astype(F32)).astype(BF16)
        both = one(jnp.concatenate([keys, query], axis=0), keys_t)
        gram, meets = both[:ROWS], both[ROWS:]
        diagonal = gram * eye
        inv_row = lax.rsqrt(jnp.sum(diagonal, axis=0, keepdims=True) + 1e-06)
        inv_col = lax.rsqrt(jnp.sum(diagonal, axis=1, keepdims=True) + 1e-06)
        query_f = query.astype(F32)
        inv_query = lax.rsqrt(jnp.sum(query_f * query_f, axis=1, keepdims=True) + 1e-06)
        lower = jnp.where(
            (seg_col == seg_row) & (row > col),
            (beta_col * inv_col) * jnp.exp(cum_col - cum_row) * (gram * inv_row),
            0.0,
        )
        scores = jnp.where(
            (seg_tok == seg_row) & (col_tok <= 2 * row_tok + 1),
            inv_query * jnp.exp(cum_tok - cum_row) * (meets * inv_row),
            0.0,
        )
        entry_row = jnp.where(seg_row == start, jnp.exp(cum_row), 0.0)
        entry_tok = jnp.where(seg_tok == start, jnp.exp(cum_tok), 0.0)
        tail_col = jnp.where(seg_col == last_seg, jnp.exp(cum_last - cum_col), 0.0)
        tail_entry = jnp.where(last_seg == start, jnp.exp(cum_last), 0.0)
        prepared.append(
            dict(
                keys=keys,
                keys_t=keys_t,
                lower=lower,
                scores=scores,
                value_scale=beta_row,
                key_scale=beta_row * entry_row * inv_row,
                tail=tail_col * inv_col,
                tail_entry=tail_entry,
                reach=(entry_tok * inv_query) * query_f,
            )
        )

    inverses = [eye - jnp.where(apart < 2, p["lower"], 0.0) for p in prepared]
    size = 2
    lowers = [p["lower"].astype(BF16) for p in prepared]
    nothing = jnp.zeros((ROWS, ROWS), BF16)
    while size < ROWS:
        below = (row > col) & (apart >= size) & (apart < 2 * size)
        rounded = [x.astype(BF16) for x in inverses]
        masked = [jnp.where(below, low, nothing) for low in lowers]
        if size < 16:
            inner = [one(m, x).astype(BF16) for m, x in zip(masked, rounded)]
            inverses = [x - one(r, i) for x, r, i in zip(inverses, rounded, inner)]
        else:
            inner = [one(lower_rows(m, size), x).astype(BF16) for m, x in zip(masked, rounded)]
            inner = [spread_rows(i, size) for i in inner]
            change = [one(lower_rows(r, size), i) for r, i in zip(rounded, inner)]
            inverses = [x - spread_rows(c, size) for x, c in zip(inverses, change)]
        size *= 2
    for _ in range(REFINES):
        sided = [beside_halves(x) for x in inverses]
        off = [eye - x - mul_sided(beside_halves(p["lower"]), s) for x, p, s in zip(inverses, prepared, sided)]
        inverses = [x + one(s[:, :ROWS], o.astype(BF16)) for x, s, o in zip(inverses, sided, off)]

    solved = []
    for (which, block), p, x in zip(units, prepared, inverses):
        values = v_ref[block * ROWS : (block + 1) * ROWS, which * DV : (which + 1) * DV]
        key_mix = one(beside_halves(x * p["key_scale"]), under(p["keys"]))
        pseudo = one(beside_halves(x * p["value_scale"]), under(values))
        solved.append(jnp.concatenate([key_mix, pseudo], axis=1))
    reads = []
    for p, s in zip(prepared, solved):
        s_hi, s_lo = halves(s)
        score_hi, score_lo = halves(p["scores"])
        both = one(jnp.concatenate([score_hi, score_lo], axis=0), s_hi)
        reads.append(both[:GROUP] + both[GROUP:] + one(score_hi, s_lo))
    moves = []
    for p, s in zip(prepared, solved):
        twice = jnp.concatenate([p["keys_t"], p["keys_t"]], axis=1)
        moves.append(one(twice, jnp.concatenate(halves(s * p["tail"]), axis=0)))
    running = [None] * HEADS_STEP
    for block in range(blocks):
        for which in range(HEADS_STEP):
            at = which * blocks + block
            p, toks = prepared[at], slice(block * GROUP, (block + 1) * GROUP)
            reach = p["reach"] - reads[at][:, :DK]
            block_map = p["tail_entry"] * eye - moves[at][:, :DK]
            if block == 0:
                mapped, local = reach, reads[at][:, DK:]
                running[which] = jnp.concatenate([block_map, moves[at][:, DK:]], axis=1)
            else:
                out = mul_wide(jnp.concatenate([reach, block_map], axis=0), running[which])
                mapped, local = out[:GROUP, :DK], out[:GROUP, DK:] + reads[at][:, DK:]
                running[which] = jnp.concatenate(
                    [out[GROUP:, :DK], out[GROUP:, DK:] + moves[at][:, DK:]], axis=1
                )
            mapped_ref[which, toks, :] = beside_halves(mapped)
            local_ref[which, toks, :] = local
    for which in range(HEADS_STEP):
        map_ref[which] = beside_halves(jnp.transpose(running[which][:, :DK]))
        add_ref[which] = jnp.transpose(running[which][:, DK:])
    segs = seg_ref[...].astype(F32)
    edge_ref[0] = jnp.broadcast_to(segs[:, 0:1], (8, 128))
    edge_ref[1] = jnp.broadcast_to(segs[:, segs.shape[1] - 1 :], (8, 128))


def local_parts(queries, keys, values, betas, log_decay, segment):
    tok_local = queries.shape[0]
    heads_local = betas.shape[1]
    lanes = HEADS_STEP * DK
    whole = lambda *shape: pl.BlockSpec(shape, lambda h: (0,) * len(shape))
    per_head = lambda rows, width: pl.BlockSpec((HEADS_STEP, rows, width), lambda h: (h, 0, 0))
    shape = lambda rows, width, dtype: jax.ShapeDtypeStruct((heads_local, rows, width), dtype)
    return pl.pallas_call(
        local_kernel,
        grid=(heads_local // HEADS_STEP,),
        in_specs=[
            pl.BlockSpec((tok_local, lanes), lambda h: (0, h)),
            pl.BlockSpec((2 * tok_local, lanes), lambda h: (0, h)),
            pl.BlockSpec((2 * tok_local, lanes), lambda h: (0, h)),
            whole(2, heads_local, tok_local),
            whole(heads_local, tok_local),
            whole(1, tok_local),
        ],
        out_specs=[
            per_head(DK, 2 * DK),
            per_head(DV, DK),
            per_head(tok_local, 2 * DK),
            per_head(tok_local, DV),
            whole(2, 8, 128),
        ],
        out_shape=[
            shape(DK, 2 * DK, BF16),
            shape(DV, DK, F32),
            shape(tok_local, 2 * DK, BF16),
            shape(tok_local, DV, F32),
            jax.ShapeDtypeStruct((2, 8, 128), F32),
        ],
        compiler_params=pltpu.CompilerParams(vmem_limit_bytes=48 * 1024 * 1024),
        cost_estimate=pl.CostEstimate(flops=12 * 10**9, bytes_accessed=8 * 10**6, transcendentals=10**6),
        name="local_blocks",
    )(
        queries,
        keys.reshape(2 * tok_local, -1),
        values.reshape(2 * tok_local, -1),
        betas,
        log_decay,
        segment.reshape(1, tok_local),
    )


MESH = pl.DeviceIdType.MESH
CHUNK = 256
PIECES = 2


def finish_kernel(
    map_ref, add_ref, mapped_ref, local_ref, edge_ref, gain_ref, weight_ref, out_ref,
    weight, normed, states, leaving, seg_in, outgoing, incoming, total, summed,
    weight_sem, seg_send, seg_recv, chain_send, chain_recv, pair_send, pair_recv, far_send, far_recv,
):
    place, places = lax.axis_index("ctx"), lax.axis_size("ctx")
    mine = lax.axis_index("head")
    heads = map_ref.shape[0]
    width = out_ref.shape[1]
    chunks = width // CHUNK
    rows = DV // PIECES
    beside = mine + 1 - 2 * lax.rem(mine, 2)
    across = lax.rem(mine + 2, 4)
    diagonal = 3 - mine
    after, before = place + 1, place - 1
    has_after, has_before = place < places - 1, place > 0

    fetch = pltpu.make_async_copy(weight_ref, weight, weight_sem)
    fetch.start()
    barrier = pltpu.get_barrier_semaphore()
    for partner in (beside, across):
        pl.semaphore_signal(barrier, inc=1, device_id=(place, partner), device_id_type=MESH)

    @pl.when(has_after)
    def _():
        pl.semaphore_signal(barrier, inc=1, device_id=(after, mine), device_id_type=MESH)

    @pl.when(has_before)
    def _():
        pl.semaphore_signal(barrier, inc=1, device_id=(before, mine), device_id_type=MESH)

    pl.semaphore_wait(barrier, 2 + has_after.astype(jnp.int32) + has_before.astype(jnp.int32))

    seg_copy = pltpu.make_async_remote_copy(
        src_ref=edge_ref.at[1], dst_ref=seg_in, send_sem=seg_send, recv_sem=seg_recv,
        device_id=(after, mine), device_id_type=MESH,
    )

    def state_copy(head, piece):
        return pltpu.make_async_remote_copy(
            src_ref=leaving.at[head, piece], dst_ref=states.at[head, piece],
            send_sem=chain_send.at[head, piece], recv_sem=chain_recv.at[head, piece],
            device_id=(after, mine), device_id_type=MESH,
        )

    def attend(head, state):
        attended = local_ref[head]
        if state is not None:
            attended = attended + mul_sided(mapped_ref[head], beside_halves(jnp.transpose(state)))
        inverse_rms = 1.0 / jnp.sqrt(jnp.mean(attended * attended, axis=-1, keepdims=True) + 1e-06)
        lanes = pl.ds(pl.multiple_of(head * DV, DV), DV)
        normed[:, lanes] = (attended * inverse_rms * gain_ref[:, lanes]).astype(BF16)

    @pl.when(place == 0)
    def _():
        seg_copy.start()

        def first(head, carry):
            for piece in range(PIECES):
                leaving[head, piece] = add_ref[head, piece * rows : (piece + 1) * rows, :]
                state_copy(head, piece).start()
            return carry

        lax.fori_loop(0, heads, first, 0)

        def read(head, carry):
            attend(head, None)
            return carry

        lax.fori_loop(0, heads, read, 0)

    @pl.when(has_before)
    def _():
        @pl.when(has_after)
        def _():
            seg_copy.start()

        seg_copy.wait_recv()
        linked = seg_in[0:1, :] == edge_ref[0, 0:1, :]

        def link(head, carry):
            carried = map_ref[head]
            whole = []
            for piece in range(PIECES):
                added = add_ref[head, piece * rows : (piece + 1) * rows, :]
                state_copy(head, piece).wait_recv()
                state = jnp.where(linked, states[head, piece], 0.0)
                whole.append(state)

                @pl.when(has_after)
                def _():
                    leaving[head, piece] = mul_sided(beside_halves(state), carried) + added
                    state_copy(head, piece).start()

            attend(head, jnp.concatenate(whole, axis=0))
            return carry

        lax.fori_loop(0, heads, link, 0)

    fetch.wait()

    def product(owner, chunk):
        lanes = pl.ds(pl.multiple_of(owner * width + chunk * CHUNK, CHUNK), CHUNK)
        return one(normed[...], weight[:, lanes])

    def pair_copy(near, chunk):
        return pltpu.make_async_remote_copy(
            src_ref=outgoing.at[near, chunk], dst_ref=incoming.at[near, chunk],
            send_sem=pair_send.at[near, chunk], recv_sem=pair_recv.at[near, chunk],
            device_id=(place, beside), device_id_type=MESH,
        )

    def far_copy(chunk):
        return pltpu.make_async_remote_copy(
            src_ref=total.at[0, chunk], dst_ref=summed.at[chunk],
            send_sem=far_send.at[chunk], recv_sem=far_recv.at[chunk],
            device_id=(place, across), device_id_type=MESH,
        )

    for near, theirs, ours in ((0, diagonal, across), (1, beside, mine)):

        def give(chunk, carry):
            outgoing[near, chunk] = product(theirs, chunk)
            pair_copy(near, chunk).start()
            return carry

        def take(chunk, carry):
            part = product(ours, chunk)
            pair_copy(near, chunk).wait_recv()
            total[near, chunk] = part + incoming[near, chunk]
            if near == 0:
                far_copy(chunk).start()
            return carry

        lax.fori_loop(0, chunks, give, 0)
        lax.fori_loop(0, chunks, take, 0)

    for chunk in range(chunks):
        far_copy(chunk).wait_recv()
        out_ref[:, chunk * CHUNK : (chunk + 1) * CHUNK] = (total[1, chunk] + summed[chunk]).astype(BF16)

    for chunk in range(chunks):
        far_copy(chunk).wait_send()
        for near in range(2):
            pair_copy(near, chunk).wait_send()

    @pl.when(has_after)
    def _():
        seg_copy.wait_send()

        def sent(head, carry):
            for piece in range(PIECES):
                state_copy(head, piece).wait_send()
            return carry

        lax.fori_loop(0, heads, sent, 0)


def finish(maps, adds, mapped, local_out, edges, gain, out_weight):
    heads, tok_local = mapped.shape[:2]
    width = out_weight.shape[1] // lax.axis_size("head")
    chunks = width // CHUNK
    dma = pltpu.SemaphoreType.DMA
    vmem = pl.BlockSpec(memory_space=pltpu.VMEM)
    return pl.pallas_call(
        finish_kernel,
        out_shape=jax.ShapeDtypeStruct((tok_local, width), BF16),
        in_specs=[vmem] * 6 + [pl.BlockSpec(memory_space=pl.ANY)],
        out_specs=vmem,
        scratch_shapes=[
            pltpu.VMEM(out_weight.shape, BF16),
            pltpu.VMEM((tok_local, heads * DV), BF16),
            pltpu.VMEM((heads, PIECES, DV // PIECES, DK), F32),
            pltpu.VMEM((heads, PIECES, DV // PIECES, DK), F32),
            pltpu.VMEM((8, 128), F32),
            pltpu.VMEM((2, chunks, tok_local, CHUNK), F32),
            pltpu.VMEM((2, chunks, tok_local, CHUNK), F32),
            pltpu.VMEM((2, chunks, tok_local, CHUNK), F32),
            pltpu.VMEM((chunks, tok_local, CHUNK), F32),
            dma,
            dma,
            dma,
            dma((heads, PIECES)),
            dma((heads, PIECES)),
            dma((2, chunks)),
            dma((2, chunks)),
            dma((chunks,)),
            dma((chunks,)),
        ],
        compiler_params=pltpu.CompilerParams(
            vmem_limit_bytes=48 * 1024 * 1024, collective_id=0, has_side_effects=True
        ),
        cost_estimate=pl.CostEstimate(flops=4 * 10**9, bytes_accessed=14 * 10**6, transcendentals=10**4),
        name="chain_and_project",
    )(maps, adds, mapped, local_out, edges, gain, out_weight)


def shards(queries, keys, values, betas, log_decay, segment, gain, out_weight):
    parts = local_parts(queries, keys, values, betas, log_decay, segment)
    return finish(*parts, gain.reshape(1, -1), out_weight)


def solution(mesh):
    return jax.shard_map(
        shards,
        mesh=mesh,
        in_specs=(
            P("ctx", "head"),
            P("ctx", None, "head"),
            P("ctx", None, "head"),
            P(None, "head", "ctx"),
            P("head", "ctx"),
            P("ctx"),
            P("head"),
            P("head", None),
        ),
        out_specs=P("ctx", "head"),
        check_vma=False,
    )
```

```python
import functools
import jax
import jax.numpy as jnp
from jax import lax
from jax.experimental import pallas as pl
from jax.experimental.pallas import tpu as pltpu
from jax.sharding import PartitionSpec as P

DK = 128
DV = 128
GROUP = 64
ROWS = 2 * GROUP
HEADS_STEP = 4
REFINES = 2
F32 = jnp.float32
BF16 = jnp.bfloat16


def halves(a):
    if a.dtype == BF16:
        return a, None
    hi = a.astype(BF16)
    return hi, (a - hi.astype(F32)).astype(BF16)


def one(a, b):
    return jnp.dot(a, b, preferred_element_type=F32)


def beside_halves(a):
    return jnp.concatenate(halves(a), axis=1)


def under(b):
    return jnp.concatenate([b, b], axis=0)


def folded(product):
    half = product.shape[1] // 2
    return product[:, :half] + product[:, half:]


def mul_sided(a_sided, b_sided):
    return folded(one(a_sided, under(b_sided)))


def mul_wide(a, b):
    a_hi, a_lo = halves(a)
    b_hi, b_lo = halves(b)
    both = one(jnp.concatenate([a_hi, a_lo], axis=0), b_hi)
    return both[: a.shape[0]] + both[a.shape[0] :] + one(a_hi, b_lo)


def lower_rows(a, size):
    return jnp.concatenate(
        [a[at + size : at + 2 * size] for at in range(0, ROWS, 2 * size)], axis=0
    )


def spread_rows(a, size):
    zero = jnp.zeros((size, a.shape[1]), a.dtype)
    return jnp.concatenate(
        [part for at in range(0, ROWS // 2, size) for part in (zero, a[at : at + size])], axis=0
    )


def exact(a, b):
    return lax.dot_general(
        a, b, (((1,), (0,)), ((), ())), precision=lax.Precision.HIGHEST, preferred_element_type=F32
    )


def local_kernel(
    q_ref, k_ref, v_ref, beta_ref, log_ref, seg_ref, map_ref, add_ref, mapped_ref, local_ref, edge_ref
):
    step = pl.program_id(0)
    blocks = q_ref.shape[0] // GROUP
    row = lax.broadcasted_iota(jnp.int32, (ROWS, ROWS), 0)
    col = lax.broadcasted_iota(jnp.int32, (ROWS, ROWS), 1)
    row_tok = lax.broadcasted_iota(jnp.int32, (GROUP, ROWS), 0)
    col_tok = lax.broadcasted_iota(jnp.int32, (GROUP, ROWS), 1)
    eye = (row == col).astype(F32)
    apart = row ^ col
    half_col = col >> 1
    summing = ((row < GROUP) & (row <= half_col)).astype(F32)
    spreading = ((row < GROUP) & (row == half_col)).astype(F32)
    weaving = jnp.where(
        row < GROUP, (col == 2 * row).astype(F32), (col == 2 * (row - GROUP) + 1).astype(F32)
    )
    units = [(which, block) for which in range(HEADS_STEP) for block in range(blocks)]
    segs = seg_ref[...].astype(F32)
    zero = jnp.zeros((1, GROUP), F32)
    log_rows, beta_rows, seg_rows = [], [], []
    for which, block in units:
        head, toks = step * HEADS_STEP + which, slice(block * GROUP, (block + 1) * GROUP)
        log_row = log_ref[pl.ds(head, 1), :]
        first, second = (beta_ref[j, pl.ds(head, 1), :] for j in range(2))
        log_rows.append(jnp.concatenate([log_row[:, toks], zero], axis=1))
        beta_rows.append(jnp.concatenate([first[:, toks], second[:, toks]], axis=1))
        seg_rows.append(jnp.concatenate([segs[:, toks], zero], axis=1))
    count = len(units)
    log_rows, beta_rows, seg_rows = (jnp.concatenate(r, axis=0) for r in (log_rows, beta_rows, seg_rows))
    cum_rows = exact(log_rows, summing)
    strength_rows = exact(beta_rows, weaving)
    doc_rows = exact(seg_rows, spreading)
    tok_rows = exact(log_rows, ((row < GROUP) & (row <= col)).astype(F32))
    columns = jnp.transpose(
        jnp.concatenate(
            [cum_rows, strength_rows, doc_rows, tok_rows, seg_rows]
            + [jnp.zeros((ROWS - 5 * count, ROWS), F32)],
            axis=0,
        )
    )

    prepared = []
    for at, (which, block) in enumerate(units):
        toks = slice(block * GROUP, (block + 1) * GROUP)
        cum_row, beta_row, seg_row = (r[at : at + 1] for r in (cum_rows, strength_rows, doc_rows))
        cum_col, beta_col, seg_col, cum_tok, seg_tok = (
            columns[:, k * count + at : k * count + at + 1] for k in range(5)
        )
        cum_tok, seg_tok = cum_tok[:GROUP], seg_tok[:GROUP]
        start = segs[:, 0:1] if block == 0 else segs[:, block * GROUP - 1 : block * GROUP]
        last_seg = segs[:, (block + 1) * GROUP - 1 : (block + 1) * GROUP]
        cum_last = cum_row[:, ROWS - 1 : ROWS]

        lanes = slice(which * DK, (which + 1) * DK)
        keys = k_ref[block * ROWS : (block + 1) * ROWS, lanes]
        query = q_ref[toks, lanes]
        keys_t = jnp.transpose(keys.astype(F32)).astype(BF16)
        both = one(jnp.concatenate([keys, query], axis=0), keys_t)
        gram, meets = both[:ROWS], both[ROWS:]
        diagonal = gram * eye
        inv_row = lax.rsqrt(jnp.sum(diagonal, axis=0, keepdims=True) + 1e-06)
        inv_col = lax.rsqrt(jnp.sum(diagonal, axis=1, keepdims=True) + 1e-06)
        query_f = query.astype(F32)
        inv_query = lax.rsqrt(jnp.sum(query_f * query_f, axis=1, keepdims=True) + 1e-06)
        lower = jnp.where(
            (seg_col == seg_row) & (row > col),
            (beta_col * inv_col) * jnp.exp(cum_col - cum_row) * (gram * inv_row),
            0.0,
        )
        scores = jnp.where(
            (seg_tok == seg_row) & (col_tok <= 2 * row_tok + 1),
            inv_query * jnp.exp(cum_tok - cum_row) * (meets * inv_row),
            0.0,
        )
        entry_row = jnp.where(seg_row == start, jnp.exp(cum_row), 0.0)
        entry_tok = jnp.where(seg_tok == start, jnp.exp(cum_tok), 0.0)
        tail_col = jnp.where(seg_col == last_seg, jnp.exp(cum_last - cum_col), 0.0)
        tail_entry = jnp.where(last_seg == start, jnp.exp(cum_last), 0.0)
        prepared.append(
            dict(
                keys=keys,
                keys_t=keys_t,
                lower=lower,
                scores=scores,
                value_scale=beta_row,
                key_scale=beta_row * entry_row * inv_row,
                tail=tail_col * inv_col,
                tail_entry=tail_entry,
                reach=(entry_tok * inv_query) * query_f,
            )
        )

    inverses = [eye - jnp.where(apart < 2, p["lower"], 0.0) for p in prepared]
    size = 2
    lowers = [p["lower"].astype(BF16) for p in prepared]
    while size < ROWS:
        below = (row > col) & (apart >= size) & (apart < 2 * size)
        rounded = [x.astype(BF16) for x in inverses]
        kept = below.astype(F32).astype(BF16)
        masked = [low * kept for low in lowers]
        if size < 16:
            inner = [one(m, x).astype(BF16) for m, x in zip(masked, rounded)]
            inverses = [x - one(r, i) for x, r, i in zip(inverses, rounded, inner)]
        else:
            inner = [one(lower_rows(m, size), x).astype(BF16) for m, x in zip(masked, rounded)]
            inner = [spread_rows(i, size) for i in inner]
            change = [one(lower_rows(r, size), i) for r, i in zip(rounded, inner)]
            inverses = [x - spread_rows(c, size) for x, c in zip(inverses, change)]
        size *= 2
    for _ in range(REFINES):
        sided = [beside_halves(x) for x in inverses]
        off = [eye - x - mul_sided(beside_halves(p["lower"]), s) for x, p, s in zip(inverses, prepared, sided)]
        inverses = [x + one(s[:, :ROWS], o.astype(BF16)) for x, s, o in zip(inverses, sided, off)]

    solved = []
    for (which, block), p, x in zip(units, prepared, inverses):
        values = v_ref[block * ROWS : (block + 1) * ROWS, which * DV : (which + 1) * DV]
        key_mix = one(beside_halves(x * p["key_scale"]), under(p["keys"]))
        pseudo = one(beside_halves(x * p["value_scale"]), under(values))
        solved.append(jnp.concatenate([key_mix, pseudo], axis=1))
    reads = []
    for p, s in zip(prepared, solved):
        s_hi, s_lo = halves(s)
        score_hi, score_lo = halves(p["scores"])
        both = one(jnp.concatenate([score_hi, score_lo], axis=0), s_hi)
        reads.append(both[:GROUP] + both[GROUP:] + one(score_hi, s_lo))
    moves = []
    for p, s in zip(prepared, solved):
        twice = jnp.concatenate([p["keys_t"], p["keys_t"]], axis=1)
        moves.append(one(twice, jnp.concatenate(halves(s * p["tail"]), axis=0)))
    running = [None] * HEADS_STEP
    for block in range(blocks):
        for which in range(HEADS_STEP):
            at = which * blocks + block
            p, toks = prepared[at], slice(block * GROUP, (block + 1) * GROUP)
            reach = p["reach"] - reads[at][:, :DK]
            block_map = p["tail_entry"] * eye - moves[at][:, :DK]
            if block == 0:
                mapped, local = reach, reads[at][:, DK:]
                running[which] = jnp.concatenate([block_map, moves[at][:, DK:]], axis=1)
            else:
                out = mul_wide(jnp.concatenate([reach, block_map], axis=0), running[which])
                mapped, local = out[:GROUP, :DK], out[:GROUP, DK:] + reads[at][:, DK:]
                running[which] = jnp.concatenate(
                    [out[GROUP:, :DK], out[GROUP:, DK:] + moves[at][:, DK:]], axis=1
                )
            mapped_ref[which, toks, :] = beside_halves(mapped)
            local_ref[which, toks, :] = local
    for which in range(HEADS_STEP):
        map_ref[which] = beside_halves(jnp.transpose(running[which][:, :DK]))
        add_ref[which] = jnp.transpose(running[which][:, DK:])
    segs = seg_ref[...].astype(F32)
    edge_ref[0] = jnp.broadcast_to(segs[:, 0:1], (8, 128))
    edge_ref[1] = jnp.broadcast_to(segs[:, segs.shape[1] - 1 :], (8, 128))


def local_parts(queries, keys, values, betas, log_decay, segment):
    tok_local = queries.shape[0]
    heads_local = betas.shape[1]
    lanes = HEADS_STEP * DK
    whole = lambda *shape: pl.BlockSpec(shape, lambda h: (0,) * len(shape))
    per_head = lambda rows, width: pl.BlockSpec((HEADS_STEP, rows, width), lambda h: (h, 0, 0))
    shape = lambda rows, width, dtype: jax.ShapeDtypeStruct((heads_local, rows, width), dtype)
    return pl.pallas_call(
        local_kernel,
        grid=(heads_local // HEADS_STEP,),
        in_specs=[
            pl.BlockSpec((tok_local, lanes), lambda h: (0, h)),
            pl.BlockSpec((2 * tok_local, lanes), lambda h: (0, h)),
            pl.BlockSpec((2 * tok_local, lanes), lambda h: (0, h)),
            whole(2, heads_local, tok_local),
            whole(heads_local, tok_local),
            whole(1, tok_local),
        ],
        out_specs=[
            per_head(DK, 2 * DK),
            per_head(DV, DK),
            per_head(tok_local, 2 * DK),
            per_head(tok_local, DV),
            whole(2, 8, 128),
        ],
        out_shape=[
            shape(DK, 2 * DK, BF16),
            shape(DV, DK, F32),
            shape(tok_local, 2 * DK, BF16),
            shape(tok_local, DV, F32),
            jax.ShapeDtypeStruct((2, 8, 128), F32),
        ],
        compiler_params=pltpu.CompilerParams(vmem_limit_bytes=48 * 1024 * 1024),
        cost_estimate=pl.CostEstimate(flops=12 * 10**9, bytes_accessed=8 * 10**6, transcendentals=10**6),
        name="local_blocks",
    )(
        queries,
        keys.reshape(2 * tok_local, -1),
        values.reshape(2 * tok_local, -1),
        betas,
        log_decay,
        segment.reshape(1, tok_local),
    )


MESH = pl.DeviceIdType.MESH
CHUNK = 256
PIECES = 2


def finish_kernel(
    map_ref, add_ref, mapped_ref, local_ref, edge_ref, gain_ref, weight_ref, out_ref,
    weight, normed, states, leaving, seg_in, outgoing, incoming, total, summed,
    weight_sem, seg_send, seg_recv, chain_send, chain_recv, pair_send, pair_recv, far_send, far_recv,
):
    place, places = lax.axis_index("ctx"), lax.axis_size("ctx")
    mine = lax.axis_index("head")
    heads = map_ref.shape[0]
    width = out_ref.shape[1]
    chunks = width // CHUNK
    rows = DV // PIECES
    beside = mine + 1 - 2 * lax.rem(mine, 2)
    across = lax.rem(mine + 2, 4)
    diagonal = 3 - mine
    after, before = place + 1, place - 1
    has_after, has_before = place < places - 1, place > 0

    fetch = pltpu.make_async_copy(weight_ref, weight, weight_sem)
    fetch.start()
    barrier = pltpu.get_barrier_semaphore()
    for partner in (beside, across):
        pl.semaphore_signal(barrier, inc=1, device_id=(place, partner), device_id_type=MESH)

    @pl.when(has_after)
    def _():
        pl.semaphore_signal(barrier, inc=1, device_id=(after, mine), device_id_type=MESH)

    @pl.when(has_before)
    def _():
        pl.semaphore_signal(barrier, inc=1, device_id=(before, mine), device_id_type=MESH)

    pl.semaphore_wait(barrier, 2 + has_after.astype(jnp.int32) + has_before.astype(jnp.int32))

    seg_copy = pltpu.make_async_remote_copy(
        src_ref=edge_ref.at[1], dst_ref=seg_in, send_sem=seg_send, recv_sem=seg_recv,
        device_id=(after, mine), device_id_type=MESH,
    )

    def state_copy(head, piece):
        return pltpu.make_async_remote_copy(
            src_ref=leaving.at[head, piece], dst_ref=states.at[head, piece],
            send_sem=chain_send.at[head, piece], recv_sem=chain_recv.at[head, piece],
            device_id=(after, mine), device_id_type=MESH,
        )

    def attend(head, state):
        attended = local_ref[head]
        if state is not None:
            attended = attended + mul_sided(mapped_ref[head], beside_halves(jnp.transpose(state)))
        inverse_rms = 1.0 / jnp.sqrt(jnp.mean(attended * attended, axis=-1, keepdims=True) + 1e-06)
        lanes = pl.ds(pl.multiple_of(head * DV, DV), DV)
        normed[:, lanes] = (attended * inverse_rms * gain_ref[:, lanes]).astype(BF16)

    @pl.when(place == 0)
    def _():
        seg_copy.start()

        def first(head, carry):
            for piece in range(PIECES):
                leaving[head, piece] = add_ref[head, piece * rows : (piece + 1) * rows, :]
                state_copy(head, piece).start()
            return carry

        lax.fori_loop(0, heads, first, 0)

        def read(head, carry):
            attend(head, None)
            return carry

        lax.fori_loop(0, heads, read, 0)

    @pl.when(has_before)
    def _():
        @pl.when(has_after)
        def _():
            seg_copy.start()

        seg_copy.wait_recv()
        linked = seg_in[0:1, :] == edge_ref[0, 0:1, :]

        def link(head, carry):
            carried = map_ref[head]
            whole = []
            for piece in range(PIECES):
                added = add_ref[head, piece * rows : (piece + 1) * rows, :]
                state_copy(head, piece).wait_recv()
                state = jnp.where(linked, states[head, piece], 0.0)
                whole.append(state)

                @pl.when(has_after)
                def _():
                    leaving[head, piece] = mul_sided(beside_halves(state), carried) + added
                    state_copy(head, piece).start()

            attend(head, jnp.concatenate(whole, axis=0))
            return carry

        lax.fori_loop(0, heads, link, 0)

    fetch.wait()

    def product(owner, chunk):
        lanes = pl.ds(pl.multiple_of(owner * width + chunk * CHUNK, CHUNK), CHUNK)
        return one(normed[...], weight[:, lanes])

    def pair_copy(near, chunk):
        return pltpu.make_async_remote_copy(
            src_ref=outgoing.at[near, chunk], dst_ref=incoming.at[near, chunk],
            send_sem=pair_send.at[near, chunk], recv_sem=pair_recv.at[near, chunk],
            device_id=(place, beside), device_id_type=MESH,
        )

    def far_copy(chunk):
        return pltpu.make_async_remote_copy(
            src_ref=total.at[0, chunk], dst_ref=summed.at[chunk],
            send_sem=far_send.at[chunk], recv_sem=far_recv.at[chunk],
            device_id=(place, across), device_id_type=MESH,
        )

    for near, theirs, ours in ((0, diagonal, across), (1, beside, mine)):

        def give(chunk, carry):
            outgoing[near, chunk] = product(theirs, chunk)
            pair_copy(near, chunk).start()
            return carry

        def take(chunk, carry):
            part = product(ours, chunk)
            pair_copy(near, chunk).wait_recv()
            total[near, chunk] = part + incoming[near, chunk]
            if near == 0:
                far_copy(chunk).start()
            return carry

        lax.fori_loop(0, chunks, give, 0)
        lax.fori_loop(0, chunks, take, 0)

    for chunk in range(chunks):
        far_copy(chunk).wait_recv()
        out_ref[:, chunk * CHUNK : (chunk + 1) * CHUNK] = (total[1, chunk] + summed[chunk]).astype(BF16)

    for chunk in range(chunks):
        far_copy(chunk).wait_send()
        for near in range(2):
            pair_copy(near, chunk).wait_send()

    @pl.when(has_after)
    def _():
        seg_copy.wait_send()

        def sent(head, carry):
            for piece in range(PIECES):
                state_copy(head, piece).wait_send()
            return carry

        lax.fori_loop(0, heads, sent, 0)


def finish(maps, adds, mapped, local_out, edges, gain, out_weight):
    heads, tok_local = mapped.shape[:2]
    width = out_weight.shape[1] // lax.axis_size("head")
    chunks = width // CHUNK
    dma = pltpu.SemaphoreType.DMA
    vmem = pl.BlockSpec(memory_space=pltpu.VMEM)
    return pl.pallas_call(
        finish_kernel,
        out_shape=jax.ShapeDtypeStruct((tok_local, width), BF16),
        in_specs=[vmem] * 6 + [pl.BlockSpec(memory_space=pl.ANY)],
        out_specs=vmem,
        scratch_shapes=[
            pltpu.VMEM(out_weight.shape, BF16),
            pltpu.VMEM((tok_local, heads * DV), BF16),
            pltpu.VMEM((heads, PIECES, DV // PIECES, DK), F32),
            pltpu.VMEM((heads, PIECES, DV // PIECES, DK), F32),
            pltpu.VMEM((8, 128), F32),
            pltpu.VMEM((2, chunks, tok_local, CHUNK), F32),
            pltpu.VMEM((2, chunks, tok_local, CHUNK), F32),
            pltpu.VMEM((2, chunks, tok_local, CHUNK), F32),
            pltpu.VMEM((chunks, tok_local, CHUNK), F32),
            dma,
            dma,
            dma,
            dma((heads, PIECES)),
            dma((heads, PIECES)),
            dma((2, chunks)),
            dma((2, chunks)),
            dma((chunks,)),
            dma((chunks,)),
        ],
        compiler_params=pltpu.CompilerParams(
            vmem_limit_bytes=48 * 1024 * 1024, collective_id=0, has_side_effects=True
        ),
        cost_estimate=pl.CostEstimate(flops=4 * 10**9, bytes_accessed=14 * 10**6, transcendentals=10**4),
        name="chain_and_project",
    )(maps, adds, mapped, local_out, edges, gain, out_weight)


def shards(queries, keys, values, betas, log_decay, segment, gain, out_weight):
    parts = local_parts(queries, keys, values, betas, log_decay, segment)
    return finish(*parts, gain.reshape(1, -1), out_weight)


def solution(mesh):
    return jax.shard_map(
        shards,
        mesh=mesh,
        in_specs=(
            P("ctx", "head"),
            P("ctx", None, "head"),
            P("ctx", None, "head"),
            P(None, "head", "ctx"),
            P("head", "ctx"),
            P("ctx"),
            P("head"),
            P("head", None),
        ),
        out_specs=P("ctx", "head"),
        check_vma=False,
    )
```
